32 devices in a mesh: dp: 2 (over x), tp: 4 (over y, core), ep: 4 (over z).
Axes of the slice: x: 2, y: 2, z: 4, core: 2. Of those that a mesh axis runs over, the one named last changes fastest.
Arguments:
- queries: bfloat16 [24, 128, 576], P(('dp', 'ep'), 'tp'), may hold values from -24 to 24
- cache: bfloat16 [192, 128, 576], P(('dp', 'tp', 'ep')), may hold values from -12 to 12
- tables: int32 [32, 6], P(('dp', 'tp', 'ep')), may hold values from 0 to 5, each once within a row
- lengths: int32 [2, 4, 3], P('dp', 'ep'), may hold values from 1 to 1024, 2048 in all within a row
- mig_cache: bfloat16 [64, 128, 576], P(('dp', 'tp', 'ep')), may hold values from -12 to 12
- mig_src: int32 [4], P('ep'), may hold values from 0 to 1
- mig_dst: int32 [4], P('ep'), may hold values from 0 to 1, as said below
- mig_seq: int32 [4], P('ep'), may hold values from 0 to 2
- tokens: bfloat16 [512, 3584], P(('dp', 'tp', 'ep')), may hold values from -6 to 6
- routes: int32 [512, 2], P(('dp', 'tp', 'ep')), may hold values from 0 to 3, all different within a row; in each aligned block of 16 rows (0 to 15, 16 to 31, ...) at most 16 rows name the same one
- gates: float32 [512, 2], P(('dp', 'tp', 'ep')), may hold values from 0.1 to 1
- gate_w: bfloat16 [4, 3584, 2048], P('ep', None, ('dp', 'tp')), may hold values from -0.09375 to 0.09375
- up_w: bfloat16 [4, 3584, 2048], P('ep', None, ('dp', 'tp')), may hold values from -0.09375 to 0.09375
- down_w: bfloat16 [4, 2048, 3584], P('ep', None, ('dp', 'tp')), may hold values from -0.125 to 0.125
Outputs:
- attn_out: bfloat16 [24, 128, 512], P(('dp', 'ep'), 'tp')
- moe_out: bfloat16 [512, 3584], P(('dp', 'tp', 'ep'))
The draws below stay inside these ranges and needn't reach their ends.
Inputs may be any that keep to these rules, and one draw needn't show every extreme that they name: `tables`: each device's row is an ordering of its 6 page ids. The lengths of each group's 3 requests sum to 2048. `mig_dst`: differs from mig_src at every index. `routes`: each row names 2 different experts; in the rows of one device no expert is named more than 16 times, a bound that some block reaches.
All inputs are finite; a program needn't handle non-finite values.
Results may differ from the reference program's by a relative error of at most 0.0058.
Values may be sent and summed in bfloat16 or wider, within the bound.
A program may use at most 64 MiB of HBM per device.

```python
import math
import jax
import jax.numpy as jnp
import numpy as np
from jax import lax

D = 3584
FF_E = 2048
HEADS = 128
KV_RANK = 512
ROPE_DIM = 64
PAGE = 128
SLOTS = 2
SEQS_G = 3
TOK_DEV = 16
TOP_WIN = 2
PAGES_DEV = 6
MAXLEN = 1024
CAP = 16
N_DP = 2
N_TP = 4
N_EP = 4
DEVICES = 32


def normal_rows(key, count):
    values = jax.random.normal(key, (count, PAGE, KV_RANK + ROPE_DIM), jnp.float32)
    return jnp.clip(values, -4.0, 4.0)


def migration_pair(key):
    source = jax.random.randint(jax.random.fold_in(key, 91), (N_EP,), 0, N_DP, dtype=jnp.int32)
    offset = jax.random.randint(jax.random.fold_in(key, 92), (N_EP,), 1, N_DP, dtype=jnp.int32)
    return (source, (source + offset) % N_DP)


def draw_queries(key, part):
    key = jax.random.fold_in(key, 17)
    key_main = jax.random.fold_in(key, 1)
    count = N_DP * N_EP * SEQS_G
    values = jnp.clip(jax.random.normal(key_main, (count, HEADS, KV_RANK + ROPE_DIM), jnp.float32), -4.0, 4.0)
    return values.astype(jnp.bfloat16)


def draw_cache(key, part):
    key = jax.random.fold_in(key, 21)
    values = normal_rows(jax.random.fold_in(key, 5), DEVICES * PAGES_DEV)
    return values.astype(jnp.bfloat16)


def draw_mig_cache(key, part):
    key = jax.random.fold_in(key, 23)
    values = normal_rows(jax.random.fold_in(key, 5), DEVICES * SLOTS)
    return values.astype(jnp.bfloat16)


def draw_mig_src(key, part):
    source, target = migration_pair(key)
    return source


def draw_mig_dst(key, part):
    source, target = migration_pair(key)
    return target


def plant(entries, own_key, low, high):
    spot = [jax.random.randint(jax.random.fold_in(own_key, axis), (), 0, length) for axis, length in enumerate(entries.shape)]
    longest = entries.shape.index(max(entries.shape))
    next_to = spot[:longest] + [(spot[longest] + 1) % entries.shape[longest]] + spot[longest + 1:]
    return entries.at[tuple(spot)].set(low).at[tuple(next_to)].set(high)


def block_scale(key, extent, cuts, smallest, high):
    def one(position, blocks):
        heights = jax.random.uniform(jax.random.fold_in(jax.random.fold_in(key, 6), position), (blocks,), jnp.float32, smallest / len(cuts), high / len(cuts))
        return jnp.repeat(jnp.exp(heights), extent[position] // blocks).reshape((-1,) + (1,) * (len(extent) - position - 1))

    factor_of = one(*cuts[0])
    for cut in cuts[1:]:
        factor_of = factor_of * one(*cut)
    return factor_of


def profile(amount, total, bound, slope):
    portions = [(1 << 20) // math.isqrt(grade ** slope) + 1 for grade in range(2, amount + 1)]
    spare, holding = total - bound - (amount - 1), [1] * (amount - 1)
    while spare > 0:
        free = [i for i in range(amount - 1) if holding[i] < bound]
        mass, remaining = sum([portions[i] for i in free]), spare
        for i in free:
            more = min(bound - holding[i], max(1, remaining * portions[i] // mass), spare)
            holding[i] = holding[i] + more
            spare = spare - more
    return np.array([bound] + holding)


def ragged_sizes(rng, count, total, reach, slope):
    if count == 2:
        one = jax.random.randint(rng, (), max(1, total - reach), min(reach, total - 1) + 1)
        return jnp.stack([one, total - one])
    sizes = jnp.asarray(profile(count, total, reach, slope), jnp.int32)
    couples = (count - 1) // 2
    source_of, receiver = sizes[1:1 + 2 * couples:2], sizes[2:2 + 2 * couples:2]
    margin = jnp.minimum(source_of - 1, reach - receiver)
    moved = jax.random.randint(jax.random.fold_in(rng, 1), (couples,), 0, 1 << 20) % (margin + 1)
    sizes = sizes.at[1:1 + 2 * couples:2].set(source_of - moved).at[2:2 + 2 * couples:2].set(receiver + moved)
    return sizes[jax.random.permutation(jax.random.fold_in(rng, 2), count)]


def shared_out(rng, own, number, rows, number_of, top, most, skew):
    sequence = jax.random.permutation(rng, number_of)
    crowded, ordinary = shares(number_of, rows * top, most, skew, True), shares(number_of, rows * top, most, skew, False)
    places = jnp.arange(number_of)

    def named(sizes, turn):
        used = int((sizes > 0).sum())
        fixed = max(1, used // 4)
        passed = fixed + (places - fixed + turn * (used - fixed)) % max(1, number_of - fixed)
        return jnp.zeros((number_of,), jnp.int32).at[sequence[jnp.where(places < fixed, places, passed)]].set(jnp.asarray(sizes, jnp.int32))

    sizes = jnp.where(number % 4 == 0, named(crowded, number // 4), named(ordinary, number - number // 4 - 1))
    mixed = jax.random.permutation(jax.random.fold_in(own, 3), number_of)
    source_of, receiver = mixed[0:number_of // 2 * 2:2], mixed[1:number_of // 2 * 2:2]
    margin = jnp.minimum(sizes[source_of] - 1, most - sizes[receiver]) // 2
    margin = jnp.where((source_of == sequence[0]) | (receiver == sequence[0]) | (sizes[receiver] == 0), 0, jnp.maximum(margin, 0))
    passed = jax.random.randint(jax.random.fold_in(own, 4), (number_of // 2,), 0, 1 << 20) % (margin + 1)
    sizes = sizes.at[source_of].add(-passed).at[receiver].add(passed)
    items = jnp.searchsorted(jnp.cumsum(sizes), jnp.arange(rows * top), side="right").astype(jnp.int32)
    listing = items.reshape(top, rows).T
    listing = listing[jax.random.permutation(jax.random.fold_in(own, 1), rows)]
    turn = jax.random.randint(jax.random.fold_in(own, 2), (rows, 1), 0, top)
    return jnp.take_along_axis(listing, (jnp.arange(top)[None, :] + turn) % top, axis=1)


def shares(amount, total, reach, lean, full):
    portions = [(1 << 20) // math.isqrt(rank ** lean) + 1 for rank in range(1, amount + 1)]
    largest = reach if full else min(reach, max(-(-total // amount), total * portions[0] // sum(portions)))
    least = 1 if total - largest >= amount - 1 else 0
    counts, rest = [largest] + [least] * (amount - 1), total - largest - least * (amount - 1)
    while rest > 0:
        candidates = [i for i in range(1, amount) if counts[i] < largest] or [i for i in range(1, amount) if counts[i] < reach]
        whole, left = sum([portions[i] for i in candidates]), rest
        for i in candidates:
            extra = min(reach - counts[i], max(1, left * portions[i] // whole), rest)
            counts[i] = counts[i] + extra
            rest = rest - extra
    return np.array(counts)


def bell_draw(rng, extent, scale, reach, pieces=(), kind=jnp.bfloat16):
    entries = jax.random.normal(rng, extent, jnp.float32) * scale
    if len(pieces) > 0:
        entries = block_scale(rng, extent, pieces, -0.22, 0.18) * entries
    return jnp.clip(entries, min=-reach, max=reach).astype(kind)


def setup_inputs(seed: int = 0) -> dict:
    splits = jax.random.split(jax.random.key(seed), 15)
    queries = draw_queries(jax.random.fold_in(splits[14], 71), 0)
    cache = draw_cache(jax.random.fold_in(splits[14], 71), 0)
    tables = jax.vmap(lambda own: jax.random.permutation(own, PAGES_DEV))(jax.random.split(splits[2], (N_DP * N_TP * N_EP))).reshape((N_DP * N_TP * N_EP, PAGES_DEV)).astype(jnp.int32)
    lengths = jax.vmap(lambda own: ragged_sizes(own, SEQS_G, 2 * MAXLEN, MAXLEN, 2))(jax.random.split(splits[3], N_DP * N_EP)).reshape((N_DP, N_EP, SEQS_G)).astype(jnp.int32)
    mig_cache = draw_mig_cache(jax.random.fold_in(splits[14], 71), 0)
    mig_src = draw_mig_src(jax.random.fold_in(splits[14], 71), 0)
    mig_dst = draw_mig_dst(jax.random.fold_in(splits[14], 71), 0)
    mig_seq = plant(jax.random.randint(splits[7], (N_EP,), 0, SEQS_G), jax.random.fold_in(splits[7], 1), 0, SEQS_G - 1).astype(jnp.int32)
    tokens = bell_draw(splits[8], (N_DP * N_TP * N_EP * TOK_DEV, D), 1.0, 6.0, ((0, 32),))
    routes_keys = jax.random.split(jax.random.fold_in(splits[9], 1), (N_DP * N_TP * N_EP * TOK_DEV) // TOK_DEV)
    routes_turns = jax.random.permutation(jax.random.fold_in(splits[9], 3), (N_DP * N_TP * N_EP * TOK_DEV) // TOK_DEV)
    routes = jax.vmap(lambda own, number: shared_out(jax.random.fold_in(splits[9], 2), own, number, TOK_DEV, N_EP, TOP_WIN, CAP, 2))(routes_keys, routes_turns).reshape((N_DP * N_TP * N_EP * TOK_DEV, TOP_WIN))
    gates = jnp.clip(jnp.exp(math.log(1.0) - 2.3025851 * jax.random.uniform(splits[10], (N_DP * N_TP * N_EP * TOK_DEV, TOP_WIN), jnp.float32) ** block_scale(splits[10], (N_DP * N_TP * N_EP * TOK_DEV, TOP_WIN), ((0, 32),), -0.2, 0.2)), 0.1, 1.0)
    gate_w = bell_draw(splits[11], (N_EP, D, FF_E), D ** -0.5, 0.09375, ((0, 4), (2, 8)))
    up_w = bell_draw(splits[12], (N_EP, D, FF_E), D ** -0.5, 0.09375, ((0, 4), (2, 8)))
    down_w = bell_draw(splits[13], (N_EP, FF_E, D), FF_E ** -0.5, 0.125, ((0, 4), (2, 8)))
    return {"queries": queries, "cache": cache, "tables": tables, "lengths": lengths, "mig_cache": mig_cache, "mig_src": mig_src, "mig_dst": mig_dst, "mig_seq": mig_seq, "tokens": tokens, "routes": routes, "gates": gates, "gate_w": gate_w, "up_w": up_w, "down_w": down_w}


score_scale = 0.07216878364870322
neg_fill = -1.0e30


def group_attention(query_group, key_parts, valid):
    scores = jnp.einsum('shc,tskc->tshk', query_group.astype(jnp.float32), key_parts.astype(jnp.float32)) * score_scale
    masked = jnp.where(valid[:, :, None, :], scores, neg_fill)
    part_max = jnp.max(masked, axis=3)
    weights = jnp.where(valid[:, :, None, :], jnp.exp(masked - part_max[..., None]), 0.0).astype(jnp.bfloat16)
    part_sum = jnp.sum(weights.astype(jnp.float32), axis=3)
    part_acc = jnp.einsum('tshk,tskc->tshc', weights.astype(jnp.float32), key_parts[..., :KV_RANK].astype(jnp.float32))
    most = jnp.max(part_max, axis=0)
    factor = jnp.exp(part_max - most)
    numerator = jnp.sum(part_acc * factor[..., None], axis=0)
    denominator = jnp.sum(part_sum * factor, axis=0)
    return (numerator / denominator[..., None]).astype(jnp.bfloat16)


def route_places(route_ids):
    flattened_index_list = route_ids.reshape(-1)
    matches = (flattened_index_list[:, None] == jnp.arange(N_EP)[None, :]).astype(jnp.int32)
    before = jnp.cumsum(matches, axis=0) - matches
    column = flattened_index_list * CAP + jnp.sum(before * matches, axis=1)
    return (column[:, None] == jnp.arange(N_EP * CAP)[None, :]).reshape(TOK_DEV, TOP_WIN, N_EP * CAP)


def reference(queries, cache, tables, lengths, mig_cache, mig_src, mig_dst, mig_seq, tokens, routes, gates, gate_w, up_w, down_w):
    row_width = KV_RANK + ROPE_DIM
    query_blocks = queries.reshape(N_DP, N_EP, SEQS_G, HEADS, row_width)
    page_pools = cache.reshape(N_DP, N_TP, N_EP, PAGES_DEV, PAGE, row_width)
    table_blocks = tables.reshape(N_DP, N_TP, N_EP, SEQS_G, SLOTS)
    moved_pages = mig_cache.reshape(N_DP, N_TP, N_EP, SLOTS, PAGE, row_width)
    positions = ((jnp.arange(SLOTS)[None, :, None] * N_TP + jnp.arange(N_TP)[:, None, None]) * PAGE
                 + jnp.arange(PAGE)[None, None, :]).reshape(N_TP, SLOTS * PAGE)

    def one_group(index):
        dp_index = index // N_EP
        ep_index = index % N_EP
        query_group = query_blocks[dp_index, ep_index]
        pools = page_pools[dp_index, :, ep_index]
        picks = table_blocks[dp_index, :, ep_index]
        own_pages = jax.vmap(lambda page_pool, page_index_list: page_pool[page_index_list])(pools, picks)
        incoming = moved_pages[mig_src[ep_index], :, ep_index]
        chosen = (dp_index == mig_dst[ep_index]) & (jnp.arange(SEQS_G) == mig_seq[ep_index])
        key_parts = jnp.where(chosen[None, :, None, None, None], incoming[:, None], own_pages)
        key_parts = key_parts.reshape(N_TP, SEQS_G, SLOTS * PAGE, row_width)
        valid = positions[:, None, :] < lengths[dp_index, ep_index][None, :, None]
        return group_attention(query_group, key_parts, valid)

    grouped = lax.map(one_group, jnp.arange(N_DP * N_EP))
    attn_out = grouped.reshape(N_DP * N_EP * SEQS_G, HEADS, KV_RANK)

    devices_all = N_DP * N_TP * N_EP
    width = tokens.shape[1]
    places = jax.vmap(route_places)(routes.reshape(devices_all, TOK_DEV, TOP_WIN))
    selected_entries = jnp.any(places, axis=2).astype(jnp.float32)
    token_block_table = tokens.reshape(devices_all, TOK_DEV, width)
    dispatched_rows = jnp.einsum('cit,cip->ctp', selected_entries, token_block_table.astype(jnp.float32)).astype(jnp.bfloat16)
    expert_rows = dispatched_rows.reshape(devices_all, N_EP, CAP, width).transpose(1, 0, 2, 3).reshape(N_EP, devices_all * CAP, width)

    def one_expert(operands):
        rows_in, weight_gate, weight_up, weight_down = operands
        rows_wide = rows_in.astype(jnp.float32)
        gate = jnp.dot(rows_wide, weight_gate.astype(jnp.float32), preferred_element_type=jnp.float32)
        upward = jnp.dot(rows_wide, weight_up.astype(jnp.float32), preferred_element_type=jnp.float32)
        hidden = (jax.nn.silu(gate) * upward).astype(jnp.bfloat16)
        return jnp.dot(hidden.astype(jnp.float32), weight_down.astype(jnp.float32), preferred_element_type=jnp.float32).astype(jnp.bfloat16)

    expert_out = lax.map(one_expert, (expert_rows, gate_w, up_w, down_w))
    returned = expert_out.reshape(N_EP, devices_all, CAP, width).transpose(1, 0, 2, 3).reshape(devices_all, N_EP * CAP, width)
    chosen_rows = jnp.einsum('drkm,dmf->drkf', places.astype(jnp.float32), returned.astype(jnp.float32))
    mixed = jnp.sum(chosen_rows * gates.reshape(devices_all, TOK_DEV, TOP_WIN)[..., None], axis=2)
    moe_out = mixed.reshape(devices_all * TOK_DEV, width).astype(jnp.bfloat16)
    return (attn_out, moe_out)
```

```python
import jax
import jax.numpy as jnp
from jax import lax
from jax.experimental import pallas as pl
from jax.experimental.pallas import tpu as pltpu
from jax.sharding import PartitionSpec as P

KV_RANK = 512
ROPE_DIM = 64
PAGE = 128
SLOTS = 2


score_scale = 0.07216878364870322
neg_fill = -1e30


def broadcast(x, axis, root):
    mine = lax.axis_index(axis) == root
    return lax.psum(jnp.where(mine, x, jnp.zeros_like(x)), axis)


def per_device(
    queries,
    cache,
    tables,
    lengths,
    mig_cache,
    mig_src,
    mig_dst,
    mig_seq,
    tokens,
    routes,
    gates,
    gate_w,
    up_w,
    down_w,
):
    tensor_parallel_ranks = lax.axis_size("tp")
    rank_tp = lax.axis_index("tp")
    rank_dp = lax.axis_index("dp")
    row_width = KV_RANK + ROPE_DIM
    group_query = lax.all_gather(queries, "tp", axis=1, tiled=True)
    seqs_group = group_query.shape[0]
    moved_pages = broadcast(mig_cache, "dp", mig_src[0])
    own_pages = cache[tables.reshape(seqs_group, SLOTS)]
    chosen = (rank_dp == mig_dst[0]) & (jnp.arange(seqs_group) == mig_seq[0])
    key_rows = jnp.where(chosen[:, None, None, None], moved_pages[None], own_pages)
    key_rows = key_rows.reshape(seqs_group, SLOTS * PAGE, row_width)
    positions = (
        (jnp.arange(SLOTS)[:, None] * tensor_parallel_ranks + rank_tp) * PAGE
        + jnp.arange(PAGE)[None, :]
    ).reshape(-1)
    valid = positions[None, :] < lengths[0, 0][:, None]
    scores = (
        jnp.einsum("shc,skc->shk", group_query, key_rows, preferred_element_type=jnp.float32)
        * score_scale
    )
    masked = jnp.where(valid[:, None, :], scores, neg_fill)
    part_max = jnp.max(masked, axis=2)
    weights = jnp.where(valid[:, None, :], jnp.exp(masked - part_max[..., None]), 0.0).astype(
        jnp.bfloat16
    )
    part_sum = jnp.sum(weights.astype(jnp.float32), axis=2)
    part_acc = jnp.einsum(
        "shk,skc->shc", weights, key_rows[:, :, :KV_RANK], preferred_element_type=jnp.float32
    )
    most = lax.pmax(part_max, "tp")
    factor = jnp.exp(part_max - most)
    numerator, denominator = (
        lax.psum_scatter(part_acc * factor[..., None], "tp", scatter_dimension=1, tiled=True),
        lax.psum_scatter(part_sum * factor, "tp", scatter_dimension=1, tiled=True),
    )
    attn_out = (numerator / denominator[..., None]).astype(jnp.bfloat16)
    ranks_ep = lax.axis_size("ep")
    token_rows = tokens.shape[0]
    top_routes = routes.shape[1]
    width = tokens.shape[1]
    capacity = min(token_rows, max(2, 2 * token_rows * top_routes // ranks_ep))
    slots_all = ranks_ep * capacity
    flattened_index_list = routes.reshape(-1)
    matches = (flattened_index_list[:, None] == jnp.arange(ranks_ep)[None, :]).astype(jnp.int32)
    before = jnp.cumsum(matches, axis=0) - matches
    column = flattened_index_list * capacity + jnp.sum(before * matches, axis=1)
    places = (column[:, None] == jnp.arange(slots_all)[None, :]).reshape(
        token_rows, top_routes, slots_all
    )
    selected_entries = jnp.any(places, axis=1).astype(jnp.bfloat16)
    dispatched_rows = lax.dot_general(
        selected_entries, tokens, (((0,), (0,)), ((), ())), preferred_element_type=jnp.float32
    )
    dispatched_rows = dispatched_rows.astype(jnp.bfloat16).reshape(ranks_ep, capacity, width)
    weight_gate = gate_w[0]
    weight_up = up_w[0]
    weight_down = down_w[0]
    arrived = lax.all_to_all(dispatched_rows, "ep", split_axis=0, concat_axis=0, tiled=True)
    piece = lax.all_gather(arrived[None], ("dp", "tp"), axis=0, tiled=True)
    piece_rows = piece.reshape(-1, width)
    gate = jnp.dot(piece_rows, weight_gate, preferred_element_type=jnp.float32)
    upward = jnp.dot(piece_rows, weight_up, preferred_element_type=jnp.float32)
    hidden_piece = (jax.nn.silu(gate) * upward).astype(jnp.bfloat16)
    hidden = hidden_piece.reshape(piece.shape[:-1] + (weight_gate.shape[1],))
    group_size = hidden.shape[0]
    total_rows = group_size * slots_all
    output_column_slice = weight_down.shape[1]
    summed = jnp.dot(
        lax.all_gather(hidden, ("dp", "tp"), axis=3, tiled=True).reshape(total_rows, -1),
        weight_down,
        preferred_element_type=jnp.float32,
    )
    expert_out = summed.astype(jnp.bfloat16)
    full_rows = lax.all_to_all(
        expert_out.reshape(group_size, slots_all, output_column_slice),
        ("dp", "tp"),
        split_axis=0,
        concat_axis=2,
        tiled=True,
    )
    returned = lax.all_to_all(
        full_rows.reshape(ranks_ep, capacity, width), "ep", split_axis=0, concat_axis=0, tiled=True
    )
    returned_rows = returned.reshape(slots_all, width)
    mixed = jnp.zeros((token_rows, width), jnp.float32)
    for route in range(top_routes):
        chosen_rows = jnp.dot(
            places[:, route].astype(jnp.bfloat16), returned_rows, preferred_element_type=jnp.float32
        )
        mixed = mixed + gates[:, route : route + 1] * chosen_rows
    return (attn_out, mixed.astype(jnp.bfloat16))


MESH = pl.DeviceIdType.MESH
PLANE = 8
LAYERS = 4


def window_kernel(
    tables_ref,
    lengths_ref,
    mig_ref,
    queries_ref,
    cache_ref,
    pages_ref,
    tokens_ref,
    routes_ref,
    gates_ref,
    gate_w_ref,
    up_w_ref,
    down_w_ref,
    attn_ref,
    moe_ref,
    tok,
    hid,
    out,
    ret,
    wg,
    wu,
    wd,
    qry,
    pool,
    moved,
    part,
    part_in,
    stat,
    stat_in,
    loc_sem,
    zs,
    zr,
    ts,
    tr,
    hs,
    hr,
    os_,
    or_,
    qs,
    qr,
    ms,
    ps,
    pr,
    ss,
    sr,
):
    x = lax.axis_index("dp")
    t = lax.axis_index("tp")
    z = lax.axis_index("ep")
    y = lax.div(t, 2)
    c = lax.rem(t, 2)
    me = x * 4 + t
    ax, ay = lax.rem(x + 1 + c, 2), lax.rem(y + c, 2)
    bx, by = lax.rem(x + c, 2), lax.rem(y + 1 + c, 2)
    at, bt, st = ay * 2 + c, by * 2 + c, y * 2 + (1 - c)
    dev_a, dev_b, dev_s = (ax, at, z), (bx, bt, z), (x, st, z)
    dt = (1 - y) * 2 + c
    id_a, id_b, id_d = ax * 4 + at, bx * 4 + bt, (1 - x) * 4 + dt
    flip = 1 - 2 * c
    z_pair = lax.div(z, 2) * 2 + lax.rem(z + 1, 2)
    inner = lax.div(z + 1, 2) == 1

    def layer(i):
        return lax.rem(lax.div(z, 2) + lax.div(i, 2), 2) * 2 + lax.rem(z + i, 2)

    def remote(src, dst, send, recv, device):
        return pltpu.make_async_remote_copy(
            src_ref=src,
            dst_ref=dst,
            send_sem=send,
            recv_sem=recv,
            device_id=device,
            device_id_type=MESH,
        )

    barrier = pltpu.get_barrier_semaphore()
    world = PLANE * LAYERS

    def greet(j, carry):
        number = lax.rem(me * LAYERS + z + j, world)
        pl.semaphore_signal(
            barrier,
            inc=1,
            device_id=(
                lax.div(number, 16),
                lax.rem(lax.div(number, LAYERS), 4),
                lax.rem(number, LAYERS),
            ),
            device_id_type=MESH,
        )
        return carry

    own_block = tok.at[z, me]
    local = [
        pltpu.make_async_copy(tokens_ref, own_block, loc_sem.at[0]),
        pltpu.make_async_copy(queries_ref, qry.at[t], loc_sem.at[1]),
        pltpu.make_async_copy(cache_ref, pool, loc_sem.at[2]),
        pltpu.make_async_copy(gate_w_ref.at[0], wg, loc_sem.at[3]),
        pltpu.make_async_copy(up_w_ref.at[0], wu, loc_sem.at[4]),
        pltpu.make_async_copy(down_w_ref.at[0], wd, loc_sem.at[5]),
    ]
    for copy in local:
        copy.start()
    lax.fori_loop(1, world, greet, 0)
    pl.semaphore_wait(barrier, world - 1)

    def to_a(buf, k, send, recv):
        return remote(buf.at[k, me], buf.at[k, me], send.at[k, 0], recv.at[k, 0], dev_a)

    def to_b(buf, k, send, recv):
        return remote(buf.at[k, me], buf.at[k, me], send.at[k, 1], recv.at[k, 1], dev_b)

    def on_b(buf, k, send, recv):
        return remote(buf.at[k, id_a], buf.at[k, id_a], send.at[k, 2], recv.at[k, 2], dev_b)

    def to_s(buf, k, send, recv, n, ident):
        return remote(
            buf.at[k, ident], buf.at[k, ident], send.at[k, 3 + n], recv.at[k, 3 + n], dev_s
        )

    def from_s(buf, k, send, recv, n, ident):
        other = ident + flip
        return remote(
            buf.at[k, other], buf.at[k, other], send.at[k, 3 + n], recv.at[k, 3 + n], dev_s
        )

    def arrived(buf, k, send, recv, n, ident):
        return remote(buf.at[k, ident], buf.at[k, ident], send.at[k, n], recv.at[k, n], dev_a)

    def cast_start(*group):
        to_a(*group).start()
        to_b(*group).start()
        to_s(*group, 0, me).start()

    def cast_forward(*group):
        arrived(*group, 0, id_a).wait_recv()
        on_b(*group).start()
        to_s(*group, 1, id_a).start()
        arrived(*group, 1, id_b).wait_recv()
        to_s(*group, 2, id_b).start()

    def cast_end(*group):
        arrived(*group, 2, id_d).wait_recv()
        to_s(*group, 3, id_d).start()
        for n, ident in enumerate((me, id_b, id_a, id_d)):
            from_s(*group, n, ident).wait_recv()

    def cast_sent(*group):
        to_a(*group).wait_send()
        to_b(*group).wait_send()
        on_b(*group).wait_send()
        for n, ident in enumerate((me, id_a, id_b, id_d)):
            to_s(*group, n, ident).wait_send()

    def tok_group(i):
        return (tok, layer(i), ts, tr)

    def hid_group(i):
        return (hid, layer(i), hs, hr)

    def z_copy(k, n, target):
        return remote(tok.at[k, me], tok.at[k, me], zs.at[k, n], zr.at[k], (x, t, target))

    def out_copy(k, p):
        return remote(
            out.at[k, p],
            ret.at[z, me],
            os_.at[k, p],
            or_.at[z, me],
            (lax.div(p, 4), lax.rem(p, 4), k),
        )

    def out_send(i):
        k = layer(i)

        def send(j, carry):
            out_copy(k, lax.rem(me + j, PLANE)).start()
            return carry

        lax.fori_loop(lax.div(3 - i, 3), PLANE, send, 0)

    local[0].wait()
    z_copy(z, 0, z_pair).start()

    @pl.when(inner)
    def _():
        z_copy(z, 1, 3 - z).start()

    y_dev, x_dev = (x, dt, z), (1 - x, t, z)
    local[1].wait()
    q_far = remote(qry.at[t], qry.at[t], qs.at[0], qr.at[0], y_dev)
    q_near = remote(qry.at[t], qry.at[t], qs.at[1], qr.at[1], dev_s)
    q_far.start()
    q_near.start()
    cast_start(*tok_group(0))
    page_copy = remote(pages_ref, moved, ms.at[0], ms.at[1], x_dev)
    page_copy.start()

    remote(qry.at[dt], qry.at[dt], qs.at[0], qr.at[0], y_dev).wait_recv()
    q_pass = remote(qry.at[dt], qry.at[dt], qs.at[2], qr.at[2], dev_s)
    q_pass.start()
    cast_forward(*tok_group(0))
    remote(qry.at[st], qry.at[st], qs.at[1], qr.at[1], dev_s).wait_recv()
    sd = (1 - y) * 2 + (1 - c)
    remote(qry.at[sd], qry.at[sd], qs.at[2], qr.at[2], dev_s).wait_recv()
    local[2].wait()
    page_copy.wait_recv()

    receives = mig_ref[1] == x
    lane = lax.broadcasted_iota(jnp.int32, (HEADS_ALL, 128), 1)
    stats = jnp.zeros((HEADS_ALL, 128), jnp.float32)
    for s in range(3):
        chosen = receives & (mig_ref[2] == s)
        query = qry[:, s].reshape(HEADS_ALL, KV_RANK + ROPE_DIM)
        pages, masked = [], []
        for j in range(SLOTS):
            page = jnp.where(chosen, moved[j], pool[tables_ref[0, s * SLOTS + j]])
            score = (
                lax.dot_general(
                    query, page, (((1,), (1,)), ((), ())), preferred_element_type=jnp.float32
                )
                * score_scale
            )
            position = (j * 4 + t) * PAGE + lax.broadcasted_iota(
                jnp.int32, (HEADS_ALL, PAGE), 1
            )
            valid = position < lengths_ref[0, 0, s]
            pages.append((page, valid))
            masked.append(jnp.where(valid, score, neg_fill))
        top = jnp.max(jnp.maximum(masked[0], masked[1]), axis=1, keepdims=True)
        total = jnp.zeros((HEADS_ALL, 1), jnp.float32)
        acc = jnp.zeros((HEADS_ALL, KV_RANK), jnp.float32)
        for j in range(SLOTS):
            page, valid = pages[j]
            weight = jnp.where(valid, jnp.exp(masked[j] - top), 0.0).astype(jnp.bfloat16)
            total = total + jnp.sum(weight.astype(jnp.float32), axis=1, keepdims=True)
            acc = acc + jnp.dot(
                weight, page[:, :KV_RANK], preferred_element_type=jnp.float32
            )
        stats = jnp.where(lane == s, top, stats)
        stats = jnp.where(lane == 3 + s, total, stats)
        part[:, s] = acc.astype(jnp.bfloat16).reshape(4, HEADS_ALL // 4, KV_RANK)
    stat[...] = stats.reshape(4, HEADS_ALL // 4, 128)

    def part_copies(j):
        u = lax.rem(t + j, 4)
        device = (x, u, z)
        return (
            remote(part.at[u], part_in.at[t], ps.at[u], pr.at[t], device),
            remote(stat.at[u], stat_in.at[t], ss.at[u], sr.at[t], device),
        )

    for j in range(1, 4):
        for copy in part_copies(j):
            copy.start()

    local[3].wait()
    local[4].wait()
    local[5].wait()

    def step(i, carry):
        @pl.when(i < 3)
        def _():
            k = layer(i + 1)
            z_copy(k, 0, z_pair).wait_recv()

            @pl.when(inner)
            def _():
                first = lax.div(2 - i, 2)
                target = first * (3 - z) + (1 - first) * z_pair
                z_copy(k, 0, target).start()

            cast_start(*tok_group(i + 1))

        @pl.when(i < 4)
        def _():
            cast_end(*tok_group(i))
            k = layer(i)
            rows = tok[k].reshape(PLANE * 16, tok.shape[3])
            gate = jnp.dot(rows, wg[...], preferred_element_type=jnp.float32)
            up = jnp.dot(rows, wu[...], preferred_element_type=jnp.float32)
            hid[k, me] = (gate / (1.0 + jnp.exp(-gate)) * up).astype(jnp.bfloat16)
            cast_start(*hid_group(i))

        @pl.when(i < 3)
        def _():
            cast_forward(*tok_group(i + 1))

        @pl.when(i < 4)
        def _():
            cast_forward(*hid_group(i))

        @pl.when(i > 0)
        def _():
            cast_end(*hid_group(i - 1))
            k = layer(i - 1)
            depth = hid.shape[3]
            total = jnp.dot(
                hid[k, 0], wd[pl.ds(0, depth), :], preferred_element_type=jnp.float32
            )
            for p in range(1, PLANE):
                total = total + jnp.dot(
                    hid[k, p], wd[pl.ds(p * depth, depth), :], preferred_element_type=jnp.float32
                )
            out[k] = total.astype(jnp.bfloat16).reshape(PLANE, 16, out.shape[3])
            out_send(i - 1)

        return carry

    lax.fori_loop(0, 5, step, 0)
    keep = pltpu.make_async_copy(out.at[z, me], ret.at[z, me], loc_sem.at[6])
    keep.start()

    for j in range(1, 4):
        u = lax.rem(t + j, 4)
        remote(part.at[u], part_in.at[u], ps.at[u], pr.at[u], dev_s).wait_recv()
        remote(stat.at[u], stat_in.at[u], ss.at[u], sr.at[u], dev_s).wait_recv()
    part_in[t] = part[t]
    stat_in[t] = stat[t]
    for s in range(3):
        tops = [stat_in[u, :, s : s + 1] for u in range(4)]
        sums = [stat_in[u, :, 3 + s : 4 + s] for u in range(4)]
        most = jnp.maximum(jnp.maximum(tops[0], tops[1]), jnp.maximum(tops[2], tops[3]))
        numerator = jnp.zeros((HEADS_ALL // 4, KV_RANK), jnp.float32)
        denominator = jnp.zeros((HEADS_ALL // 4, 1), jnp.float32)
        for u in range(4):
            factor = jnp.exp(tops[u] - most)
            numerator = numerator + factor * part_in[u, s].astype(jnp.float32)
            denominator = denominator + factor * sums[u]
        attn_ref[s] = (numerator / denominator).astype(jnp.bfloat16)

    q_far.wait_send()
    q_near.wait_send()
    q_pass.wait_send()
    page_copy.wait_send()
    for j in range(1, 4):
        for copy in part_copies(j):
            copy.wait_send()
    z_copy(z, 0, z_pair).wait_send()

    @pl.when(inner)
    def _():
        z_copy(z, 1, 3 - z).wait_send()

    def drain(i, carry):
        @pl.when((i > 0) & inner)
        def _():
            z_copy(layer(i), 0, z_pair).wait_send()

        cast_sent(*tok_group(i))
        cast_sent(*hid_group(i))
        return carry

    lax.fori_loop(0, 4, drain, 0)

    def out_wait(i, carry):
        k = layer(i)

        def one(j, inside):
            p = lax.rem(me + j, PLANE)
            out_copy(k, p).wait_send()
            remote(out.at[k, p], ret.at[k, p], os_.at[k, p], or_.at[k, p], dev_s).wait_recv()
            return inside

        return lax.fori_loop(lax.div(3 - i, 3), PLANE, one, carry)

    lax.fori_loop(0, 4, out_wait, 0)
    keep.wait()
    named, scale = routes_ref[...], gates_ref[...]
    coefs = []
    for e in range(LAYERS):
        hits = jnp.where(named == e, scale, 0.0)
        coefs.append(hits[:, 0:1] + hits[:, 1:2])
    span = out.shape[3]
    for p in range(PLANE):
        mixed = coefs[0] * ret[0, p].astype(jnp.float32)
        for e in range(1, LAYERS):
            mixed = mixed + coefs[e] * ret[e, p].astype(jnp.float32)
        moe_ref[:, p * span : (p + 1) * span] = mixed.astype(jnp.bfloat16)


HEADS_ALL = 128


def window(
    queries,
    cache,
    tables,
    lengths,
    mig_cache,
    mig_src,
    mig_dst,
    mig_seq,
    tokens,
    routes,
    gates,
    gate_w,
    up_w,
    down_w,
):
    mig = jnp.concatenate([mig_src, mig_dst, mig_seq])
    rows, width = tokens.shape
    depth, span, units = gate_w.shape[2], down_w.shape[2], down_w.shape[1]
    heads, row_width = queries.shape[1], queries.shape[2]
    bf16, f32 = jnp.bfloat16, jnp.float32
    dma = pltpu.SemaphoreType.DMA
    smem = pl.BlockSpec(memory_space=pltpu.SMEM)
    vmem = pl.BlockSpec(memory_space=pltpu.VMEM)
    hbm = pl.BlockSpec(memory_space=pl.ANY)
    return pl.pallas_call(
        window_kernel,
        out_shape=(
            jax.ShapeDtypeStruct((queries.shape[0], heads, KV_RANK), bf16),
            jax.ShapeDtypeStruct((rows, width), bf16),
        ),
        in_specs=[smem] * 3 + [hbm] * 4 + [vmem] * 2 + [hbm] * 3,
        out_specs=(vmem, vmem),
        scratch_shapes=[
            pltpu.VMEM((LAYERS, PLANE, rows, width), bf16),
            pltpu.VMEM((LAYERS, PLANE, PLANE * rows, depth), bf16),
            pltpu.VMEM((LAYERS, PLANE, rows, span), bf16),
            pltpu.VMEM((LAYERS, PLANE, rows, span), bf16),
            pltpu.VMEM((width, depth), bf16),
            pltpu.VMEM((width, depth), bf16),
            pltpu.VMEM((units, span), bf16),
            pltpu.VMEM((4, 3, heads, row_width), bf16),
            pltpu.VMEM(cache.shape, bf16),
            pltpu.VMEM(mig_cache.shape, bf16),
            pltpu.VMEM((4, 3, heads, KV_RANK), bf16),
            pltpu.VMEM((4, 3, heads, KV_RANK), bf16),
            pltpu.VMEM((4, heads, 128), f32),
            pltpu.VMEM((4, heads, 128), f32),
            dma((7,)),
            dma((4, 2)),
            dma((4,)),
            dma((4, 7)),
            dma((4, 7)),
            dma((4, 7)),
            dma((4, 7)),
            dma((4, PLANE)),
            dma((4, PLANE)),
            dma((3,)),
            dma((3,)),
            dma((2,)),
            dma((4,)),
            dma((4,)),
            dma((4,)),
            dma((4,)),
        ],
        compiler_params=pltpu.CompilerParams(
            collective_id=0, has_side_effects=True, vmem_limit_bytes=48 * 1024 * 1024
        ),
    )(
        tables,
        lengths,
        mig,
        queries,
        cache,
        mig_cache,
        tokens,
        routes,
        gates,
        gate_w,
        up_w,
        down_w,
    )


def solution(mesh):
    form = per_device
    if (mesh.shape["dp"], mesh.shape["tp"], mesh.shape["ep"]) == (2, 4, LAYERS):
        form = window
    in_specs = (
        P(("dp", "ep"), "tp", None),
        P(("dp", "tp", "ep"), None, None),
        P(("dp", "tp", "ep"), None),
        P("dp", "ep", None),
        P(("dp", "tp", "ep"), None, None),
        P("ep"),
        P("ep"),
        P("ep"),
        P(("dp", "tp", "ep"), None),
        P(("dp", "tp", "ep"), None),
        P(("dp", "tp", "ep"), None),
        P("ep", None, ("dp", "tp")),
        P("ep", None, ("dp", "tp")),
        P("ep", None, ("dp", "tp")),
    )
    out_specs = (P(("dp", "ep"), "tp", None), P(("dp", "tp", "ep"), None))
    return jax.shard_map(
        form, mesh=mesh, in_specs=in_specs, out_specs=out_specs, check_vma=False
    )
```

```python
import jax
import jax.numpy as jnp
from jax import lax
from jax.experimental import pallas as pl
from jax.experimental.pallas import tpu as pltpu
from jax.sharding import PartitionSpec as P

KV_RANK = 512
ROPE_DIM = 64
PAGE = 128
SLOTS = 2


score_scale = 0.07216878364870322
neg_fill = -1e30


def broadcast(x, axis, root):
    mine = lax.axis_index(axis) == root
    return lax.psum(jnp.where(mine, x, jnp.zeros_like(x)), axis)


def per_device(
    queries,
    cache,
    tables,
    lengths,
    mig_cache,
    mig_src,
    mig_dst,
    mig_seq,
    tokens,
    routes,
    gates,
    gate_w,
    up_w,
    down_w,
):
    tensor_parallel_ranks = lax.axis_size("tp")
    rank_tp = lax.axis_index("tp")
    rank_dp = lax.axis_index("dp")
    row_width = KV_RANK + ROPE_DIM
    group_query = lax.all_gather(queries, "tp", axis=1, tiled=True)
    seqs_group = group_query.shape[0]
    moved_pages = broadcast(mig_cache, "dp", mig_src[0])
    own_pages = cache[tables.reshape(seqs_group, SLOTS)]
    chosen = (rank_dp == mig_dst[0]) & (jnp.arange(seqs_group) == mig_seq[0])
    key_rows = jnp.where(chosen[:, None, None, None], moved_pages[None], own_pages)
    key_rows = key_rows.reshape(seqs_group, SLOTS * PAGE, row_width)
    positions = (
        (jnp.arange(SLOTS)[:, None] * tensor_parallel_ranks + rank_tp) * PAGE
        + jnp.arange(PAGE)[None, :]
    ).reshape(-1)
    valid = positions[None, :] < lengths[0, 0][:, None]
    scores = (
        jnp.einsum("shc,skc->shk", group_query, key_rows, preferred_element_type=jnp.float32)
        * score_scale
    )
    masked = jnp.where(valid[:, None, :], scores, neg_fill)
    part_max = jnp.max(masked, axis=2)
    weights = jnp.where(valid[:, None, :], jnp.exp(masked - part_max[..., None]), 0.0).astype(
        jnp.bfloat16
    )
    part_sum = jnp.sum(weights.astype(jnp.float32), axis=2)
    part_acc = jnp.einsum(
        "shk,skc->shc", weights, key_rows[:, :, :KV_RANK], preferred_element_type=jnp.float32
    )
    most = lax.pmax(part_max, "tp")
    factor = jnp.exp(part_max - most)
    numerator, denominator = (
        lax.psum_scatter(part_acc * factor[..., None], "tp", scatter_dimension=1, tiled=True),
        lax.psum_scatter(part_sum * factor, "tp", scatter_dimension=1, tiled=True),
    )
    attn_out = (numerator / denominator[..., None]).astype(jnp.bfloat16)
    ranks_ep = lax.axis_size("ep")
    token_rows = tokens.shape[0]
    top_routes = routes.shape[1]
    width = tokens.shape[1]
    capacity = min(token_rows, max(2, 2 * token_rows * top_routes // ranks_ep))
    slots_all = ranks_ep * capacity
    flattened_index_list = routes.reshape(-1)
    matches = (flattened_index_list[:, None] == jnp.arange(ranks_ep)[None, :]).astype(jnp.int32)
    before = jnp.cumsum(matches, axis=0) - matches
    column = flattened_index_list * capacity + jnp.sum(before * matches, axis=1)
    places = (column[:, None] == jnp.arange(slots_all)[None, :]).reshape(
        token_rows, top_routes, slots_all
    )
    selected_entries = jnp.any(places, axis=1).astype(jnp.bfloat16)
    dispatched_rows = lax.dot_general(
        selected_entries, tokens, (((0,), (0,)), ((), ())), preferred_element_type=jnp.float32
    )
    dispatched_rows = dispatched_rows.astype(jnp.bfloat16).reshape(ranks_ep, capacity, width)
    weight_gate = gate_w[0]
    weight_up = up_w[0]
    weight_down = down_w[0]
    arrived = lax.all_to_all(dispatched_rows, "ep", split_axis=0, concat_axis=0, tiled=True)
    piece = lax.all_gather(arrived[None], ("dp", "tp"), axis=0, tiled=True)
    piece_rows = piece.reshape(-1, width)
    gate = jnp.dot(piece_rows, weight_gate, preferred_element_type=jnp.float32)
    upward = jnp.dot(piece_rows, weight_up, preferred_element_type=jnp.float32)
    hidden_piece = (jax.nn.silu(gate) * upward).astype(jnp.bfloat16)
    hidden = hidden_piece.reshape(piece.shape[:-1] + (weight_gate.shape[1],))
    group_size = hidden.shape[0]
    total_rows = group_size * slots_all
    output_column_slice = weight_down.shape[1]
    summed = jnp.dot(
        lax.all_gather(hidden, ("dp", "tp"), axis=3, tiled=True).reshape(total_rows, -1),
        weight_down,
        preferred_element_type=jnp.float32,
    )
    expert_out = summed.astype(jnp.bfloat16)
    full_rows = lax.all_to_all(
        expert_out.reshape(group_size, slots_all, output_column_slice),
        ("dp", "tp"),
        split_axis=0,
        concat_axis=2,
        tiled=True,
    )
    returned = lax.all_to_all(
        full_rows.reshape(ranks_ep, capacity, width), "ep", split_axis=0, concat_axis=0, tiled=True
    )
    returned_rows = returned.reshape(slots_all, width)
    mixed = jnp.zeros((token_rows, width), jnp.float32)
    for route in range(top_routes):
        chosen_rows = jnp.dot(
            places[:, route].astype(jnp.bfloat16), returned_rows, preferred_element_type=jnp.float32
        )
        mixed = mixed + gates[:, route : route + 1] * chosen_rows
    return (attn_out, mixed.astype(jnp.bfloat16))


MESH = pl.DeviceIdType.MESH
PLANE = 8
LAYERS = 4


def window_kernel(
    tables_ref,
    lengths_ref,
    mig_ref,
    queries_ref,
    cache_ref,
    pages_ref,
    tokens_ref,
    routes_ref,
    gates_ref,
    gate_w_ref,
    up_w_ref,
    down_w_ref,
    attn_ref,
    moe_ref,
    tok,
    hid,
    out,
    ret,
    wg,
    wu,
    wd,
    qry,
    pool,
    moved,
    part,
    part_in,
    stat,
    stat_in,
    loc_sem,
    zs,
    zr,
    ts,
    tr,
    hs,
    hr,
    os_,
    or_,
    qs,
    qr,
    ms,
    ps,
    pr,
    ss,
    sr,
):
    x = lax.axis_index("dp")
    t = lax.axis_index("tp")
    z = lax.axis_index("ep")
    y = lax.div(t, 2)
    c = lax.rem(t, 2)
    me = x * 4 + t
    ax, ay = lax.rem(x + 1 + c, 2), lax.rem(y + c, 2)
    bx, by = lax.rem(x + c, 2), lax.rem(y + 1 + c, 2)
    at, bt, st = ay * 2 + c, by * 2 + c, y * 2 + (1 - c)
    dev_a, dev_b, dev_s = (ax, at, z), (bx, bt, z), (x, st, z)
    dt = (1 - y) * 2 + c
    id_a, id_b, id_d = ax * 4 + at, bx * 4 + bt, (1 - x) * 4 + dt
    flip = 1 - 2 * c
    z_pair = lax.div(z, 2) * 2 + lax.rem(z + 1, 2)
    inner = lax.div(z + 1, 2) == 1

    def layer(i):
        return lax.rem(lax.div(z, 2) + lax.div(i, 2), 2) * 2 + lax.rem(z + i, 2)

    def remote(src, dst, send, recv, device):
        return pltpu.make_async_remote_copy(
            src_ref=src,
            dst_ref=dst,
            send_sem=send,
            recv_sem=recv,
            device_id=device,
            device_id_type=MESH,
        )

    barrier = pltpu.get_barrier_semaphore()
    world = PLANE * LAYERS

    def greet(j, carry):
        number = lax.rem(me * LAYERS + z + j, world)
        pl.semaphore_signal(
            barrier,
            inc=1,
            device_id=(
                lax.div(number, 16),
                lax.rem(lax.div(number, LAYERS), 4),
                lax.rem(number, LAYERS),
            ),
            device_id_type=MESH,
        )
        return carry

    own_block = tok.at[z, me]
    local = [
        pltpu.make_async_copy(tokens_ref, own_block, loc_sem.at[0]),
        pltpu.make_async_copy(queries_ref, qry.at[t], loc_sem.at[1]),
        pltpu.make_async_copy(cache_ref, pool, loc_sem.at[2]),
        pltpu.make_async_copy(gate_w_ref.at[0], wg, loc_sem.at[3]),
        pltpu.make_async_copy(up_w_ref.at[0], wu, loc_sem.at[4]),
        pltpu.make_async_copy(down_w_ref.at[0], wd, loc_sem.at[5]),
    ]
    for copy in local:
        copy.start()
    lax.fori_loop(1, world, greet, 0)
    pl.semaphore_wait(barrier, world - 1)

    def to_a(buf, k, send, recv):
        return remote(buf.at[k, me], buf.at[k, me], send.at[k, 0], recv.at[k, 0], dev_a)

    def to_b(buf, k, send, recv):
        return remote(buf.at[k, me], buf.at[k, me], send.at[k, 1], recv.at[k, 1], dev_b)

    def on_b(buf, k, send, recv):
        return remote(buf.at[k, id_a], buf.at[k, id_a], send.at[k, 2], recv.at[k, 2], dev_b)

    def to_s(buf, k, send, recv, n, ident):
        return remote(
            buf.at[k, ident], buf.at[k, ident], send.at[k, 3 + n], recv.at[k, 3 + n], dev_s
        )

    def from_s(buf, k, send, recv, n, ident):
        other = ident + flip
        return remote(
            buf.at[k, other], buf.at[k, other], send.at[k, 3 + n], recv.at[k, 3 + n], dev_s
        )

    def arrived(buf, k, send, recv, n, ident):
        return remote(buf.at[k, ident], buf.at[k, ident], send.at[k, n], recv.at[k, n], dev_a)

    def cast_start(*group):
        to_a(*group).start()
        to_b(*group).start()
        to_s(*group, 0, me).start()

    def cast_forward(*group):
        arrived(*group, 0, id_a).wait_recv()
        on_b(*group).start()
        to_s(*group, 1, id_a).start()
        arrived(*group, 1, id_b).wait_recv()
        to_s(*group, 2, id_b).start()

    def cast_end(*group):
        arrived(*group, 2, id_d).wait_recv()
        to_s(*group, 3, id_d).start()
        for n, ident in enumerate((me, id_b, id_a, id_d)):
            from_s(*group, n, ident).wait_recv()

    def cast_sent(*group):
        to_a(*group).wait_send()
        to_b(*group).wait_send()
        on_b(*group).wait_send()
        for n, ident in enumerate((me, id_a, id_b, id_d)):
            to_s(*group, n, ident).wait_send()

    def tok_group(i):
        return (tok, layer(i), ts, tr)

    def hid_group(i):
        return (hid, layer(i), hs, hr)

    def z_copy(k, n, target):
        return remote(tok.at[k, me], tok.at[k, me], zs.at[k, n], zr.at[k], (x, t, target))

    def out_copy(k, p):
        return remote(
            out.at[k, p],
            ret.at[z, me],
            os_.at[k, p],
            or_.at[z, me],
            (lax.div(p, 4), lax.rem(p, 4), k),
        )

    def out_send(i):
        k = layer(i)

        def send(j, carry):
            out_copy(k, lax.rem(me + j, PLANE)).start()
            return carry

        lax.fori_loop(lax.div(3 - i, 3), PLANE, send, 0)

    local[0].wait()
    z_copy(z, 0, z_pair).start()

    @pl.when(inner)
    def _():
        z_copy(z, 1, 3 - z).start()

    y_dev, x_dev = (x, dt, z), (1 - x, t, z)
    local[1].wait()
    q_far = remote(qry.at[t], qry.at[t], qs.at[0], qr.at[0], y_dev)
    q_near = remote(qry.at[t], qry.at[t], qs.at[1], qr.at[1], dev_s)
    q_far.start()
    q_near.start()
    page_copy = remote(pages_ref, moved, ms.at[0], ms.at[1], x_dev)
    q_pass = remote(qry.at[dt], qry.at[dt], qs.at[2], qr.at[2], dev_s)
    sd = (1 - y) * 2 + (1 - c)

    def part_copies(j):
        u = lax.rem(t + j, 4)
        device = (x, u, z)
        return (
            remote(part.at[u], part_in.at[t], ps.at[u], pr.at[t], device),
            remote(stat.at[u], stat_in.at[t], ss.at[u], sr.at[t], device),
        )

    def attend():
        remote(qry.at[st], qry.at[st], qs.at[1], qr.at[1], dev_s).wait_recv()
        remote(qry.at[sd], qry.at[sd], qs.at[2], qr.at[2], dev_s).wait_recv()
        local[2].wait()
        page_copy.wait_recv()
        receives = mig_ref[1] == x
        lane = lax.broadcasted_iota(jnp.int32, (HEADS_ALL, 128), 1)
        stats = jnp.zeros((HEADS_ALL, 128), jnp.float32)
        for s in range(3):
            chosen = receives & (mig_ref[2] == s)
            query = qry[:, s].reshape(HEADS_ALL, KV_RANK + ROPE_DIM)
            pages, masked = [], []
            for j in range(SLOTS):
                page = jnp.where(chosen, moved[j], pool[tables_ref[0, s * SLOTS + j]])
                score = (
                    lax.dot_general(
                        query, page, (((1,), (0,)), ((), ())), preferred_element_type=jnp.float32
                    )
                    * score_scale
                )
                position = (j * 4 + t) * PAGE + lax.broadcasted_iota(
                    jnp.int32, (HEADS_ALL, PAGE), 1
                )
                valid = position < lengths_ref[0, 0, s]
                pages.append((page, valid))
                masked.append(jnp.where(valid, score, neg_fill))
            top = jnp.max(jnp.maximum(masked[0], masked[1]), axis=1, keepdims=True)
            total = jnp.zeros((HEADS_ALL, 1), jnp.float32)
            acc = jnp.zeros((HEADS_ALL, KV_RANK), jnp.float32)
            for j in range(SLOTS):
                page, valid = pages[j]
                weight = jnp.where(valid, jnp.exp(masked[j] - top), 0.0).astype(jnp.bfloat16)
                total = total + jnp.sum(weight.astype(jnp.float32), axis=1, keepdims=True)
                acc = acc + lax.dot_general(
                    weight,
                    page[:KV_RANK],
                    (((1,), (1,)), ((), ())),
                    preferred_element_type=jnp.float32,
                )
            stats = jnp.where(lane == s, top, stats)
            stats = jnp.where(lane == 3 + s, total, stats)
            part[:, s] = acc.astype(jnp.bfloat16).reshape(4, HEADS_ALL // 4, KV_RANK)
        stat[...] = stats.reshape(4, HEADS_ALL // 4, 128)
        for j in range(1, 4):
            for copy in part_copies(j):
                copy.start()

    def step(i, carry):
        @pl.when(i == 0)
        def _():
            cast_start(*tok_group(0))

        @pl.when((i > 0) & (i < 4))
        def _():
            k = layer(i)
            z_copy(k, 0, z_pair).wait_recv()

            @pl.when(inner)
            def _():
                first = lax.div(3 - i, 2)
                target = first * (3 - z) + (1 - first) * z_pair
                z_copy(k, 0, target).start()

            cast_start(*tok_group(i))

        @pl.when((i > 0) & (i < 5))
        def _():
            cast_forward(*tok_group(i - 1))

        @pl.when(i == 1)
        def _():
            remote(qry.at[dt], qry.at[dt], qs.at[0], qr.at[0], y_dev).wait_recv()
            q_pass.start()

        @pl.when(i == 3)
        def _():
            page_copy.start()

        @pl.when(i == 2)
        def _():
            local[3].wait()
            local[4].wait()
            local[5].wait()

        @pl.when((i > 1) & (i < 6))
        def _():
            cast_end(*tok_group(i - 2))
            k = layer(i - 2)
            rows = tok[k].reshape(PLANE * 16, tok.shape[3])
            gate = jnp.dot(rows, wg[...], preferred_element_type=jnp.float32)
            up = jnp.dot(rows, wu[...], preferred_element_type=jnp.float32)
            hid[k, me] = (gate / (1.0 + jnp.exp(-gate)) * up).astype(jnp.bfloat16)
            cast_start(*hid_group(i - 2))

        @pl.when(i == 6)
        def _():
            attend()

        @pl.when((i > 2) & (i < 7))
        def _():
            cast_forward(*hid_group(i - 3))

        @pl.when(i > 3)
        def _():
            cast_end(*hid_group(i - 4))
            k = layer(i - 4)
            depth = hid.shape[3]
            total = jnp.zeros((PLANE * 16, out.shape[3]), jnp.float32)
            for p in range(PLANE):
                total = total + lax.dot_general(
                    hid[k, p],
                    wd[:, p * depth : (p + 1) * depth],
                    (((1,), (1,)), ((), ())),
                    preferred_element_type=jnp.float32,
                )
            out[k] = total.astype(jnp.bfloat16).reshape(PLANE, 16, out.shape[3])
            out_send(i - 4)

        return carry

    lax.fori_loop(0, 8, step, 0)
    keep = pltpu.make_async_copy(out.at[z, me], ret.at[z, me], loc_sem.at[6])
    keep.start()

    for j in range(1, 4):
        u = lax.rem(t + j, 4)
        remote(part.at[u], part_in.at[u], ps.at[u], pr.at[u], dev_s).wait_recv()
        remote(stat.at[u], stat_in.at[u], ss.at[u], sr.at[u], dev_s).wait_recv()
    part_in[t] = part[t]
    stat_in[t] = stat[t]
    for s in range(3):
        tops = [stat_in[u, :, s : s + 1] for u in range(4)]
        sums = [stat_in[u, :, 3 + s : 4 + s] for u in range(4)]
        most = jnp.maximum(jnp.maximum(tops[0], tops[1]), jnp.maximum(tops[2], tops[3]))
        numerator = jnp.zeros((HEADS_ALL // 4, KV_RANK), jnp.float32)
        denominator = jnp.zeros((HEADS_ALL // 4, 1), jnp.float32)
        for u in range(4):
            factor = jnp.exp(tops[u] - most)
            numerator = numerator + factor * part_in[u, s].astype(jnp.float32)
            denominator = denominator + factor * sums[u]
        attn_ref[s] = (numerator / denominator).astype(jnp.bfloat16)

    q_far.wait_send()
    q_near.wait_send()
    q_pass.wait_send()
    page_copy.wait_send()
    for j in range(1, 4):
        for copy in part_copies(j):
            copy.wait_send()
    z_copy(z, 0, z_pair).wait_send()

    @pl.when(inner)
    def _():
        z_copy(z, 1, 3 - z).wait_send()

    def drain(i, carry):
        @pl.when((i > 0) & inner)
        def _():
            z_copy(layer(i), 0, z_pair).wait_send()

        cast_sent(*tok_group(i))
        cast_sent(*hid_group(i))
        return carry

    lax.fori_loop(0, 4, drain, 0)

    def out_wait(i, carry):
        k = layer(i)

        def one(j, inside):
            p = lax.rem(me + j, PLANE)
            out_copy(k, p).wait_send()
            remote(out.at[k, p], ret.at[k, p], os_.at[k, p], or_.at[k, p], dev_s).wait_recv()
            return inside

        return lax.fori_loop(lax.div(3 - i, 3), PLANE, one, carry)

    lax.fori_loop(0, 4, out_wait, 0)
    keep.wait()
    named, scale = routes_ref[...], gates_ref[...]
    count = named.shape[1]
    same = lax.broadcasted_iota(jnp.int32, (count, count), 0) == lax.broadcasted_iota(
        jnp.int32, (count, count), 1
    )
    coefs = []
    for e in range(LAYERS):
        hits = jnp.sum(jnp.where(named == e, scale, 0.0), axis=0, keepdims=True)
        coefs.append(jnp.sum(jnp.where(same, hits, 0.0), axis=1, keepdims=True))
    span = out.shape[3]
    for p in range(PLANE):
        mixed = coefs[0] * ret[0, p].astype(jnp.float32)
        for e in range(1, LAYERS):
            mixed = mixed + coefs[e] * ret[e, p].astype(jnp.float32)
        moe_ref[:, p * span : (p + 1) * span] = mixed.astype(jnp.bfloat16)


HEADS_ALL = 128


def window(
    queries,
    cache,
    tables,
    lengths,
    mig_cache,
    mig_src,
    mig_dst,
    mig_seq,
    tokens,
    routes,
    gates,
    gate_w,
    up_w,
    down_w,
):
    mig = jnp.concatenate([mig_src, mig_dst, mig_seq])
    rows, width = tokens.shape
    depth, span, units = gate_w.shape[2], down_w.shape[2], down_w.shape[1]
    heads, row_width = queries.shape[1], queries.shape[2]
    pool, moved = jnp.swapaxes(cache, 1, 2), jnp.swapaxes(mig_cache, 1, 2)
    bf16, f32 = jnp.bfloat16, jnp.float32
    dma = pltpu.SemaphoreType.DMA
    smem = pl.BlockSpec(memory_space=pltpu.SMEM)
    vmem = pl.BlockSpec(memory_space=pltpu.VMEM)
    hbm = pl.BlockSpec(memory_space=pl.ANY)
    return pl.pallas_call(
        window_kernel,
        out_shape=(
            jax.ShapeDtypeStruct((queries.shape[0], heads, KV_RANK), bf16),
            jax.ShapeDtypeStruct((rows, width), bf16),
        ),
        in_specs=[smem] * 3 + [hbm] * 4 + [vmem] * 2 + [hbm] * 3,
        out_specs=(vmem, vmem),
        scratch_shapes=[
            pltpu.VMEM((LAYERS, PLANE, rows, width), bf16),
            pltpu.VMEM((LAYERS, PLANE, PLANE * rows, depth), bf16),
            pltpu.VMEM((LAYERS, PLANE, rows, span), bf16),
            pltpu.VMEM((LAYERS, PLANE, rows, span), bf16),
            pltpu.VMEM((width, depth), bf16),
            pltpu.VMEM((width, depth), bf16),
            pltpu.VMEM((span, units), bf16),
            pltpu.VMEM((4, 3, heads, row_width), bf16),
            pltpu.VMEM(pool.shape, bf16),
            pltpu.VMEM(moved.shape, bf16),
            pltpu.VMEM((4, 3, heads, KV_RANK), bf16),
            pltpu.VMEM((4, 3, heads, KV_RANK), bf16),
            pltpu.VMEM((4, heads, 128), f32),
            pltpu.VMEM((4, heads, 128), f32),
            dma((7,)),
            dma((4, 2)),
            dma((4,)),
            dma((4, 7)),
            dma((4, 7)),
            dma((4, 7)),
            dma((4, 7)),
            dma((4, PLANE)),
            dma((4, PLANE)),
            dma((3,)),
            dma((3,)),
            dma((2,)),
            dma((4,)),
            dma((4,)),
            dma((4,)),
            dma((4,)),
        ],
        compiler_params=pltpu.CompilerParams(
            collective_id=0, has_side_effects=True, vmem_limit_bytes=60 * 1024 * 1024
        ),
    )(
        tables,
        lengths,
        mig,
        queries,
        pool,
        moved,
        tokens,
        routes.T,
        gates.T,
        gate_w,
        up_w,
        jnp.swapaxes(down_w, 1, 2),
    )


def solution(mesh):
    form = per_device
    if (mesh.shape["dp"], mesh.shape["tp"], mesh.shape["ep"]) == (2, 4, LAYERS):
        form = window
    in_specs = (
        P(("dp", "ep"), "tp", None),
        P(("dp", "tp", "ep"), None, None),
        P(("dp", "tp", "ep"), None),
        P("dp", "ep", None),
        P(("dp", "tp", "ep"), None, None),
        P("ep"),
        P("ep"),
        P("ep"),
        P(("dp", "tp", "ep"), None),
        P(("dp", "tp", "ep"), None),
        P(("dp", "tp", "ep"), None),
        P("ep", None, ("dp", "tp")),
        P("ep", None, ("dp", "tp")),
        P("ep", None, ("dp", "tp")),
    )
    out_specs = (P(("dp", "ep"), "tp", None), P(("dp", "tp", "ep"), None))
    return jax.shard_map(
        form, mesh=mesh, in_specs=in_specs, out_specs=out_specs, check_vma=False
    )
```

```python
import functools

import jax
import jax.numpy as jnp
from jax import lax
from jax.experimental import pallas as pl
from jax.experimental.pallas import tpu as pltpu
from jax.sharding import PartitionSpec as P

KV_RANK = 512
ROPE_DIM = 64
PAGE = 128
SLOTS = 2


score_scale = 0.07216878364870322
neg_fill = -1e30


def broadcast(x, axis, root):
    mine = lax.axis_index(axis) == root
    return lax.psum(jnp.where(mine, x, jnp.zeros_like(x)), axis)


def per_device(
    queries,
    cache,
    tables,
    lengths,
    mig_cache,
    mig_src,
    mig_dst,
    mig_seq,
    tokens,
    routes,
    gates,
    gate_w,
    up_w,
    down_w,
):
    tensor_parallel_ranks = lax.axis_size("tp")
    rank_tp = lax.axis_index("tp")
    rank_dp = lax.axis_index("dp")
    row_width = KV_RANK + ROPE_DIM
    group_query = lax.all_gather(queries, "tp", axis=1, tiled=True)
    seqs_group = group_query.shape[0]
    moved_pages = broadcast(mig_cache, "dp", mig_src[0])
    own_pages = cache[tables.reshape(seqs_group, SLOTS)]
    chosen = (rank_dp == mig_dst[0]) & (jnp.arange(seqs_group) == mig_seq[0])
    key_rows = jnp.where(chosen[:, None, None, None], moved_pages[None], own_pages)
    key_rows = key_rows.reshape(seqs_group, SLOTS * PAGE, row_width)
    positions = (
        (jnp.arange(SLOTS)[:, None] * tensor_parallel_ranks + rank_tp) * PAGE
        + jnp.arange(PAGE)[None, :]
    ).reshape(-1)
    valid = positions[None, :] < lengths[0, 0][:, None]
    scores = (
        jnp.einsum("shc,skc->shk", group_query, key_rows, preferred_element_type=jnp.float32)
        * score_scale
    )
    masked = jnp.where(valid[:, None, :], scores, neg_fill)
    part_max = jnp.max(masked, axis=2)
    weights = jnp.where(valid[:, None, :], jnp.exp(masked - part_max[..., None]), 0.0).astype(
        jnp.bfloat16
    )
    part_sum = jnp.sum(weights.astype(jnp.float32), axis=2)
    part_acc = jnp.einsum(
        "shk,skc->shc", weights, key_rows[:, :, :KV_RANK], preferred_element_type=jnp.float32
    )
    most = lax.pmax(part_max, "tp")
    factor = jnp.exp(part_max - most)
    numerator, denominator = (
        lax.psum_scatter(part_acc * factor[..., None], "tp", scatter_dimension=1, tiled=True),
        lax.psum_scatter(part_sum * factor, "tp", scatter_dimension=1, tiled=True),
    )
    attn_out = (numerator / denominator[..., None]).astype(jnp.bfloat16)
    ranks_ep = lax.axis_size("ep")
    token_rows = tokens.shape[0]
    top_routes = routes.shape[1]
    width = tokens.shape[1]
    capacity = min(token_rows, max(2, 2 * token_rows * top_routes // ranks_ep))
    slots_all = ranks_ep * capacity
    flattened_index_list = routes.reshape(-1)
    matches = (flattened_index_list[:, None] == jnp.arange(ranks_ep)[None, :]).astype(jnp.int32)
    before = jnp.cumsum(matches, axis=0) - matches
    column = flattened_index_list * capacity + jnp.sum(before * matches, axis=1)
    places = (column[:, None] == jnp.arange(slots_all)[None, :]).reshape(
        token_rows, top_routes, slots_all
    )
    selected_entries = jnp.any(places, axis=1).astype(jnp.bfloat16)
    dispatched_rows = lax.dot_general(
        selected_entries, tokens, (((0,), (0,)), ((), ())), preferred_element_type=jnp.float32
    )
    dispatched_rows = dispatched_rows.astype(jnp.bfloat16).reshape(ranks_ep, capacity, width)
    weight_gate = gate_w[0]
    weight_up = up_w[0]
    weight_down = down_w[0]
    arrived = lax.all_to_all(dispatched_rows, "ep", split_axis=0, concat_axis=0, tiled=True)
    piece = lax.all_gather(arrived[None], ("dp", "tp"), axis=0, tiled=True)
    piece_rows = piece.reshape(-1, width)
    gate = jnp.dot(piece_rows, weight_gate, preferred_element_type=jnp.float32)
    upward = jnp.dot(piece_rows, weight_up, preferred_element_type=jnp.float32)
    hidden_piece = (jax.nn.silu(gate) * upward).astype(jnp.bfloat16)
    hidden = hidden_piece.reshape(piece.shape[:-1] + (weight_gate.shape[1],))
    group_size = hidden.shape[0]
    total_rows = group_size * slots_all
    output_column_slice = weight_down.shape[1]
    summed = jnp.dot(
        lax.all_gather(hidden, ("dp", "tp"), axis=3, tiled=True).reshape(total_rows, -1),
        weight_down,
        preferred_element_type=jnp.float32,
    )
    expert_out = summed.astype(jnp.bfloat16)
    full_rows = lax.all_to_all(
        expert_out.reshape(group_size, slots_all, output_column_slice),
        ("dp", "tp"),
        split_axis=0,
        concat_axis=2,
        tiled=True,
    )
    returned = lax.all_to_all(
        full_rows.reshape(ranks_ep, capacity, width), "ep", split_axis=0, concat_axis=0, tiled=True
    )
    returned_rows = returned.reshape(slots_all, width)
    mixed = jnp.zeros((token_rows, width), jnp.float32)
    for route in range(top_routes):
        chosen_rows = jnp.dot(
            places[:, route].astype(jnp.bfloat16), returned_rows, preferred_element_type=jnp.float32
        )
        mixed = mixed + gates[:, route : route + 1] * chosen_rows
    return (attn_out, mixed.astype(jnp.bfloat16))


MESH = pl.DeviceIdType.MESH
PLANE = 8
LAYERS = 4


def window_kernel(
    tables_ref,
    lengths_ref,
    mig_ref,
    queries_ref,
    cache_ref,
    pages_ref,
    tokens_ref,
    routes_ref,
    gates_ref,
    gate_w_ref,
    up_w_ref,
    down_w_ref,
    attn_ref,
    moe_ref,
    tok,
    hid,
    out,
    ret,
    wg,
    wu,
    wd,
    qry,
    pool,
    moved,
    part,
    part_in,
    stat,
    stat_in,
    loc_sem,
    zs,
    zr,
    ts,
    tr,
    hs,
    hr,
    os_,
    or_,
    qs,
    qr,
    ms,
    ps,
    pr,
    ss,
    sr,
):
    x = lax.axis_index("dp")
    t = lax.axis_index("tp")
    z = lax.axis_index("ep")
    y = lax.div(t, 2)
    c = lax.rem(t, 2)
    me = x * 4 + t
    ax, ay = lax.rem(x + 1 + c, 2), lax.rem(y + c, 2)
    bx, by = lax.rem(x + c, 2), lax.rem(y + 1 + c, 2)
    at, bt, st = ay * 2 + c, by * 2 + c, y * 2 + (1 - c)
    dev_a, dev_b, dev_s = (ax, at, z), (bx, bt, z), (x, st, z)
    dt = (1 - y) * 2 + c
    id_a, id_b, id_d = ax * 4 + at, bx * 4 + bt, (1 - x) * 4 + dt
    flip = 1 - 2 * c
    z_pair = lax.div(z, 2) * 2 + lax.rem(z + 1, 2)
    inner = lax.div(z + 1, 2) == 1

    half = lax.div(z, 2)

    def layer(i):
        first, last = lax.div(3 - i, 3), lax.div(i, 3)
        middle = 1 - first - last
        other = (2 - i) * (2 - half) + (i - 1) * (3 - 3 * half)
        return first * z + middle * other + last * z_pair

    def remote(src, dst, send, recv, device):
        return pltpu.make_async_remote_copy(
            src_ref=src,
            dst_ref=dst,
            send_sem=send,
            recv_sem=recv,
            device_id=device,
            device_id_type=MESH,
        )

    barrier = pltpu.get_barrier_semaphore()
    world = PLANE * LAYERS

    def greet(j, carry):
        number = lax.rem(me * LAYERS + z + j, world)
        pl.semaphore_signal(
            barrier,
            inc=1,
            device_id=(
                lax.div(number, 16),
                lax.rem(lax.div(number, LAYERS), 4),
                lax.rem(number, LAYERS),
            ),
            device_id_type=MESH,
        )
        return carry

    own_block = tok.at[z, me]
    local = [
        pltpu.make_async_copy(tokens_ref, own_block, loc_sem.at[0]),
        pltpu.make_async_copy(queries_ref, qry.at[t], loc_sem.at[1]),
        pltpu.make_async_copy(cache_ref, pool, loc_sem.at[2]),
        pltpu.make_async_copy(gate_w_ref.at[0], wg, loc_sem.at[3]),
        pltpu.make_async_copy(up_w_ref.at[0], wu, loc_sem.at[4]),
        pltpu.make_async_copy(down_w_ref.at[0], wd, loc_sem.at[5]),
    ]
    for copy in local:
        copy.start()
    lax.fori_loop(1, world, greet, 0)
    pl.semaphore_wait(barrier, world - 1)

    def to_a(buf, k, send, recv):
        return remote(buf.at[k, me], buf.at[k, me], send.at[k, 0], recv.at[k, 0], dev_a)

    def to_b(buf, k, send, recv):
        return remote(buf.at[k, me], buf.at[k, me], send.at[k, 1], recv.at[k, 1], dev_b)

    def on_b(buf, k, send, recv):
        return remote(buf.at[k, id_a], buf.at[k, id_a], send.at[k, 2], recv.at[k, 2], dev_b)

    def to_s(buf, k, send, recv, n, ident):
        return remote(
            buf.at[k, ident], buf.at[k, ident], send.at[k, 3 + n], recv.at[k, 3 + n], dev_s
        )

    def from_s(buf, k, send, recv, n, ident):
        other = ident + flip
        return remote(
            buf.at[k, other], buf.at[k, other], send.at[k, 3 + n], recv.at[k, 3 + n], dev_s
        )

    def arrived(buf, k, send, recv, n, ident):
        return remote(buf.at[k, ident], buf.at[k, ident], send.at[k, n], recv.at[k, n], dev_a)

    def cast_start(*group, plane=True):
        @pl.when(plane)
        def _():
            to_a(*group).start()
            to_b(*group).start()

        to_s(*group, 0, me).start()

    def cast_forward(*group, plane=True):
        arrived(*group, 0, id_a).wait_recv()

        @pl.when(plane)
        def _():
            on_b(*group).start()

        to_s(*group, 1, id_a).start()
        arrived(*group, 1, id_b).wait_recv()
        to_s(*group, 2, id_b).start()

    def cast_end(*group):
        arrived(*group, 2, id_d).wait_recv()
        to_s(*group, 3, id_d).start()
        for n, ident in enumerate((me, id_b, id_a, id_d)):
            from_s(*group, n, ident).wait_recv()

    def cast_sent(*group):
        to_a(*group).wait_send()
        to_b(*group).wait_send()
        on_b(*group).wait_send()
        for n, ident in enumerate((me, id_a, id_b, id_d)):
            to_s(*group, n, ident).wait_send()

    def tok_group(i):
        return (tok, layer(i), ts, tr)

    def hid_group(i):
        return (hid, layer(i), hs, hr)

    def z_copy(k, n, target):
        return remote(tok.at[k, me], tok.at[k, me], zs.at[k, n], zr.at[k], (x, t, target))

    def pair_copy(n, ident):
        return remote(
            tok.at[z, ident], tok.at[z, ident], ts.at[z_pair, n], tr.at[z, n], (x, t, z_pair)
        )

    def out_copy(k, p):
        return remote(
            out.at[k, p],
            ret.at[z, me],
            os_.at[k, p],
            or_.at[z, me],
            (lax.div(p, 4), lax.rem(p, 4), k),
        )

    def out_send(i):
        k = layer(i)

        def send(j, carry):
            out_copy(k, lax.rem(me + j, PLANE)).start()
            return carry

        lax.fori_loop(lax.div(3 - i, 3), PLANE, send, 0)

    local[0].wait()
    z_copy(z, 0, z_pair).start()

    @pl.when(inner)
    def _():
        z_copy(z, 1, 3 - z).start()

    y_dev, x_dev = (x, dt, z), (1 - x, t, z)
    local[1].wait()
    q_far = remote(qry.at[t], qry.at[t], qs.at[0], qr.at[0], y_dev)
    q_near = remote(qry.at[t], qry.at[t], qs.at[1], qr.at[1], dev_s)
    q_far.start()
    q_near.start()
    page_copy = remote(pages_ref, moved, ms.at[0], ms.at[1], x_dev)
    q_pass = remote(qry.at[dt], qry.at[dt], qs.at[2], qr.at[2], dev_s)
    sd = (1 - y) * 2 + (1 - c)

    def part_copies(n):
        u = (st, sd, dt)[n]
        device = (dev_s, dev_s, y_dev)[n]
        return (
            remote(part.at[u], part_in.at[n], ps.at[n], pr.at[n], device),
            remote(stat.at[u], stat_in.at[n], ss.at[n], sr.at[n], device),
        )

    def merge(mine, slots):
        tops = [stat[mine, :, 0:3]] + [stat_in[n, :, 0:3] for n in slots]
        sums = [stat[mine, :, 3:6]] + [stat_in[n, :, 3:6] for n in slots]
        most = functools.reduce(jnp.maximum, tops)
        factors = [jnp.exp(top - most) for top in tops]
        denominator = sum(f * a for f, a in zip(factors, sums))
        numerators = []
        for s in range(3):
            value = factors[0][:, s : s + 1] * part[mine, s].astype(jnp.float32)
            for factor, n in zip(factors[1:], slots):
                value = value + factor[:, s : s + 1] * part_in[n, s].astype(jnp.float32)
            numerators.append(value)
        return most, denominator, numerators

    def pass_on():
        for copy in part_copies(1):
            copy.wait_recv()
        most, denominator, numerators = merge(dt, (1,))
        stat[dt, :, 0:3] = most
        stat[dt, :, 3:6] = denominator
        for s in range(3):
            part[dt, s] = numerators[s].astype(jnp.bfloat16)
        for copy in part_copies(2):
            copy.start()

    def attend():
        remote(qry.at[st], qry.at[st], qs.at[1], qr.at[1], dev_s).wait_recv()
        remote(qry.at[sd], qry.at[sd], qs.at[2], qr.at[2], dev_s).wait_recv()
        local[2].wait()
        page_copy.wait_recv()
        receives = mig_ref[1] == x
        lane = lax.broadcasted_iota(jnp.int32, (HEADS_ALL, 128), 1)
        stats = jnp.zeros((HEADS_ALL, 128), jnp.float32)
        for s in range(3):
            chosen = receives & (mig_ref[2] == s)
            query = qry[:, s].reshape(HEADS_ALL, KV_RANK + ROPE_DIM)
            pages, masked = [], []
            for j in range(SLOTS):
                page = jnp.where(chosen, moved[j], pool[tables_ref[0, s * SLOTS + j]])
                score = (
                    lax.dot_general(
                        query, page, (((1,), (0,)), ((), ())), preferred_element_type=jnp.float32
                    )
                    * score_scale
                )
                position = (j * 4 + t) * PAGE + lax.broadcasted_iota(
                    jnp.int32, (HEADS_ALL, PAGE), 1
                )
                valid = position < lengths_ref[0, 0, s]
                pages.append((page, valid))
                masked.append(jnp.where(valid, score, neg_fill))
            top = jnp.max(jnp.maximum(masked[0], masked[1]), axis=1, keepdims=True)
            total = jnp.zeros((HEADS_ALL, 1), jnp.float32)
            acc = jnp.zeros((HEADS_ALL, KV_RANK), jnp.float32)
            for j in range(SLOTS):
                page, valid = pages[j]
                weight = jnp.where(valid, jnp.exp(masked[j] - top), 0.0).astype(jnp.bfloat16)
                total = total + jnp.sum(weight.astype(jnp.float32), axis=1, keepdims=True)
                acc = acc + lax.dot_general(
                    weight,
                    page[:KV_RANK],
                    (((1,), (1,)), ((), ())),
                    preferred_element_type=jnp.float32,
                )
            stats = jnp.where(lane == s, top, stats)
            stats = jnp.where(lane == 3 + s, total, stats)
            part[:, s] = acc.astype(jnp.bfloat16).reshape(4, HEADS_ALL // 4, KV_RANK)
        stat[...] = stats.reshape(4, HEADS_ALL // 4, 128)
        for n in (1, 0):
            for copy in part_copies(n):
                copy.start()

    def step(i, carry):
        @pl.when(i == 0)
        def _():
            cast_start(*tok_group(0))

        @pl.when((i > 0) & (i < 4))
        def _():
            k = layer(i)

            @pl.when(i < 3)
            def _():
                z_copy(k, 0, z_pair).wait_recv()

                @pl.when(inner)
                def _():
                    z_copy(k, 0, z_pair).start()

            @pl.when(i == 1)
            def _():
                z_copy(z_pair, 0, z_pair).wait_recv()

                @pl.when(inner)
                def _():
                    z_copy(z_pair, 0, 3 - z).start()

            cast_start(*tok_group(i), plane=i < 3)

        @pl.when((i > 0) & (i < 5))
        def _():
            cast_forward(*tok_group(i - 1), plane=i < 4)

        @pl.when(i == 1)
        def _():
            remote(qry.at[dt], qry.at[dt], qs.at[0], qr.at[0], y_dev).wait_recv()
            q_pass.start()

        @pl.when(i == 3)
        def _():
            page_copy.start()

        @pl.when(i == 2)
        def _():
            local[3].wait()
            local[4].wait()
            local[5].wait()

        @pl.when((i > 1) & (i < 6))
        def _():
            cast_end(*tok_group(i - 2))

            @pl.when(i == 2)
            def _():
                for n, ident in enumerate((id_a, id_b, id_d)):
                    pair_copy(n, ident).start()

            k = layer(i - 2)
            rows = tok[k].reshape(PLANE * 16, tok.shape[3])
            gate = jnp.dot(rows, wg[...], preferred_element_type=jnp.float32)
            up = jnp.dot(rows, wu[...], preferred_element_type=jnp.float32)
            hid[k, me] = (gate / (1.0 + jnp.exp(-gate)) * up).astype(jnp.bfloat16)
            cast_start(*hid_group(i - 2))

        @pl.when(i == 6)
        def _():
            attend()

        @pl.when(i == 7)
        def _():
            pass_on()

        @pl.when((i > 2) & (i < 7))
        def _():
            cast_forward(*hid_group(i - 3))

        @pl.when(i > 3)
        def _():
            cast_end(*hid_group(i - 4))
            k = layer(i - 4)
            depth = hid.shape[3]
            total = jnp.zeros((PLANE * 16, out.shape[3]), jnp.float32)
            for p in range(PLANE):
                total = total + lax.dot_general(
                    hid[k, p],
                    wd[:, p * depth : (p + 1) * depth],
                    (((1,), (1,)), ((), ())),
                    preferred_element_type=jnp.float32,
                )
            out[k] = total.astype(jnp.bfloat16).reshape(PLANE, 16, out.shape[3])
            out_send(i - 4)

        return carry

    lax.fori_loop(0, 8, step, 0)
    keep = pltpu.make_async_copy(out.at[z, me], ret.at[z, me], loc_sem.at[6])
    keep.start()

    for n in (0, 2):
        for copy in part_copies(n):
            copy.wait_recv()
    most, denominator, numerators = merge(t, (0, 2))
    for s in range(3):
        attn_ref[s] = (numerators[s] / denominator[:, s : s + 1]).astype(jnp.bfloat16)

    q_far.wait_send()
    q_near.wait_send()
    q_pass.wait_send()
    page_copy.wait_send()
    for n in range(3):
        for copy in part_copies(n):
            copy.wait_send()
    z_copy(z, 0, z_pair).wait_send()

    @pl.when(inner)
    def _():
        z_copy(z, 1, 3 - z).wait_send()

    def drain(i, carry):
        @pl.when((i > 0) & inner)
        def _():
            z_copy(layer(i), 0, z_pair).wait_send()

        cast_sent(*tok_group(i))
        cast_sent(*hid_group(i))
        return carry

    lax.fori_loop(0, 4, drain, 0)

    def out_wait(i, carry):
        k = layer(i)

        def one(j, inside):
            p = lax.rem(me + j, PLANE)
            out_copy(k, p).wait_send()
            remote(out.at[k, p], ret.at[k, p], os_.at[k, p], or_.at[k, p], dev_s).wait_recv()
            return inside

        return lax.fori_loop(lax.div(3 - i, 3), PLANE, one, carry)

    lax.fori_loop(0, 4, out_wait, 0)
    keep.wait()
    named, scale = routes_ref[...], gates_ref[...]
    count = named.shape[1]
    same = lax.broadcasted_iota(jnp.int32, (count, count), 0) == lax.broadcasted_iota(
        jnp.int32, (count, count), 1
    )
    coefs = []
    for e in range(LAYERS):
        hits = jnp.sum(jnp.where(named == e, scale, 0.0), axis=0, keepdims=True)
        coefs.append(jnp.sum(jnp.where(same, hits, 0.0), axis=1, keepdims=True))
    span = out.shape[3]
    for p in range(PLANE):
        mixed = coefs[0] * ret[0, p].astype(jnp.float32)
        for e in range(1, LAYERS):
            mixed = mixed + coefs[e] * ret[e, p].astype(jnp.float32)
        moe_ref[:, p * span : (p + 1) * span] = mixed.astype(jnp.bfloat16)


HEADS_ALL = 128


def window(
    queries,
    cache,
    tables,
    lengths,
    mig_cache,
    mig_src,
    mig_dst,
    mig_seq,
    tokens,
    routes,
    gates,
    gate_w,
    up_w,
    down_w,
):
    mig = jnp.concatenate([mig_src, mig_dst, mig_seq])
    rows, width = tokens.shape
    depth, span, units = gate_w.shape[2], down_w.shape[2], down_w.shape[1]
    heads, row_width = queries.shape[1], queries.shape[2]
    pool, moved = jnp.swapaxes(cache, 1, 2), jnp.swapaxes(mig_cache, 1, 2)
    bf16, f32 = jnp.bfloat16, jnp.float32
    dma = pltpu.SemaphoreType.DMA
    smem = pl.BlockSpec(memory_space=pltpu.SMEM)
    vmem = pl.BlockSpec(memory_space=pltpu.VMEM)
    hbm = pl.BlockSpec(memory_space=pl.ANY)
    return pl.pallas_call(
        window_kernel,
        out_shape=(
            jax.ShapeDtypeStruct((queries.shape[0], heads, KV_RANK), bf16),
            jax.ShapeDtypeStruct((rows, width), bf16),
        ),
        in_specs=[smem] * 3 + [hbm] * 4 + [vmem] * 2 + [hbm] * 3,
        out_specs=(vmem, vmem),
        scratch_shapes=[
            pltpu.VMEM((LAYERS, PLANE, rows, width), bf16),
            pltpu.VMEM((LAYERS, PLANE, PLANE * rows, depth), bf16),
            pltpu.VMEM((LAYERS, PLANE, rows, span), bf16),
            pltpu.VMEM((LAYERS, PLANE, rows, span), bf16),
            pltpu.VMEM((width, depth), bf16),
            pltpu.VMEM((width, depth), bf16),
            pltpu.VMEM((span, units), bf16),
            pltpu.VMEM((4, 3, heads, row_width), bf16),
            pltpu.VMEM(pool.shape, bf16),
            pltpu.VMEM(moved.shape, bf16),
            pltpu.VMEM((4, 3, heads, KV_RANK), bf16),
            pltpu.VMEM((3, 3, heads, KV_RANK), bf16),
            pltpu.VMEM((4, heads, 128), f32),
            pltpu.VMEM((3, heads, 128), f32),
            dma((7,)),
            dma((4, 2)),
            dma((4,)),
            dma((4, 7)),
            dma((4, 7)),
            dma((4, 7)),
            dma((4, 7)),
            dma((4, PLANE)),
            dma((4, PLANE)),
            dma((3,)),
            dma((3,)),
            dma((2,)),
            dma((3,)),
            dma((3,)),
            dma((3,)),
            dma((3,)),
        ],
        compiler_params=pltpu.CompilerParams(
            collective_id=0, has_side_effects=True, vmem_limit_bytes=58 * 1024 * 1024
        ),
    )(
        tables,
        lengths,
        mig,
        queries,
        pool,
        moved,
        tokens,
        routes.T,
        gates.T,
        gate_w,
        up_w,
        jnp.swapaxes(down_w, 1, 2),
    )


def solution(mesh):
    form = per_device
    if (mesh.shape["dp"], mesh.shape["tp"], mesh.shape["ep"]) == (2, 4, LAYERS):
        form = window
    in_specs = (
        P(("dp", "ep"), "tp", None),
        P(("dp", "tp", "ep"), None, None),
        P(("dp", "tp", "ep"), None),
        P("dp", "ep", None),
        P(("dp", "tp", "ep"), None, None),
        P("ep"),
        P("ep"),
        P("ep"),
        P(("dp", "tp", "ep"), None),
        P(("dp", "tp", "ep"), None),
        P(("dp", "tp", "ep"), None),
        P("ep", None, ("dp", "tp")),
        P("ep", None, ("dp", "tp")),
        P("ep", None, ("dp", "tp")),
    )
    out_specs = (P(("dp", "ep"), "tp", None), P(("dp", "tp", "ep"), None))
    return jax.shard_map(
        form, mesh=mesh, in_specs=in_specs, out_specs=out_specs, check_vma=False
    )
```

```python
import functools

import jax
import jax.numpy as jnp
from jax import lax
from jax.experimental import pallas as pl
from jax.experimental.pallas import tpu as pltpu
from jax.sharding import PartitionSpec as P

KV_RANK = 512
ROPE_DIM = 64
PAGE = 128
SLOTS = 2


score_scale = 0.07216878364870322
neg_fill = -1e30


def broadcast(x, axis, root):
    mine = lax.axis_index(axis) == root
    return lax.psum(jnp.where(mine, x, jnp.zeros_like(x)), axis)


def per_device(
    queries,
    cache,
    tables,
    lengths,
    mig_cache,
    mig_src,
    mig_dst,
    mig_seq,
    tokens,
    routes,
    gates,
    gate_w,
    up_w,
    down_w,
):
    tensor_parallel_ranks = lax.axis_size("tp")
    rank_tp = lax.axis_index("tp")
    rank_dp = lax.axis_index("dp")
    row_width = KV_RANK + ROPE_DIM
    group_query = lax.all_gather(queries, "tp", axis=1, tiled=True)
    seqs_group = group_query.shape[0]
    moved_pages = broadcast(mig_cache, "dp", mig_src[0])
    own_pages = cache[tables.reshape(seqs_group, SLOTS)]
    chosen = (rank_dp == mig_dst[0]) & (jnp.arange(seqs_group) == mig_seq[0])
    key_rows = jnp.where(chosen[:, None, None, None], moved_pages[None], own_pages)
    key_rows = key_rows.reshape(seqs_group, SLOTS * PAGE, row_width)
    positions = (
        (jnp.arange(SLOTS)[:, None] * tensor_parallel_ranks + rank_tp) * PAGE
        + jnp.arange(PAGE)[None, :]
    ).reshape(-1)
    valid = positions[None, :] < lengths[0, 0][:, None]
    scores = (
        jnp.einsum("shc,skc->shk", group_query, key_rows, preferred_element_type=jnp.float32)
        * score_scale
    )
    masked = jnp.where(valid[:, None, :], scores, neg_fill)
    part_max = jnp.max(masked, axis=2)
    weights = jnp.where(valid[:, None, :], jnp.exp(masked - part_max[..., None]), 0.0).astype(
        jnp.bfloat16
    )
    part_sum = jnp.sum(weights.astype(jnp.float32), axis=2)
    part_acc = jnp.einsum(
        "shk,skc->shc", weights, key_rows[:, :, :KV_RANK], preferred_element_type=jnp.float32
    )
    most = lax.pmax(part_max, "tp")
    factor = jnp.exp(part_max - most)
    numerator, denominator = (
        lax.psum_scatter(part_acc * factor[..., None], "tp", scatter_dimension=1, tiled=True),
        lax.psum_scatter(part_sum * factor, "tp", scatter_dimension=1, tiled=True),
    )
    attn_out = (numerator / denominator[..., None]).astype(jnp.bfloat16)
    ranks_ep = lax.axis_size("ep")
    token_rows = tokens.shape[0]
    top_routes = routes.shape[1]
    width = tokens.shape[1]
    capacity = min(token_rows, max(2, 2 * token_rows * top_routes // ranks_ep))
    slots_all = ranks_ep * capacity
    flattened_index_list = routes.reshape(-1)
    matches = (flattened_index_list[:, None] == jnp.arange(ranks_ep)[None, :]).astype(jnp.int32)
    before = jnp.cumsum(matches, axis=0) - matches
    column = flattened_index_list * capacity + jnp.sum(before * matches, axis=1)
    places = (column[:, None] == jnp.arange(slots_all)[None, :]).reshape(
        token_rows, top_routes, slots_all
    )
    selected_entries = jnp.any(places, axis=1).astype(jnp.bfloat16)
    dispatched_rows = lax.dot_general(
        selected_entries, tokens, (((0,), (0,)), ((), ())), preferred_element_type=jnp.float32
    )
    dispatched_rows = dispatched_rows.astype(jnp.bfloat16).reshape(ranks_ep, capacity, width)
    weight_gate = gate_w[0]
    weight_up = up_w[0]
    weight_down = down_w[0]
    arrived = lax.all_to_all(dispatched_rows, "ep", split_axis=0, concat_axis=0, tiled=True)
    piece = lax.all_gather(arrived[None], ("dp", "tp"), axis=0, tiled=True)
    piece_rows = piece.reshape(-1, width)
    gate = jnp.dot(piece_rows, weight_gate, preferred_element_type=jnp.float32)
    upward = jnp.dot(piece_rows, weight_up, preferred_element_type=jnp.float32)
    hidden_piece = (jax.nn.silu(gate) * upward).astype(jnp.bfloat16)
    hidden = hidden_piece.reshape(piece.shape[:-1] + (weight_gate.shape[1],))
    group_size = hidden.shape[0]
    total_rows = group_size * slots_all
    output_column_slice = weight_down.shape[1]
    summed = jnp.dot(
        lax.all_gather(hidden, ("dp", "tp"), axis=3, tiled=True).reshape(total_rows, -1),
        weight_down,
        preferred_element_type=jnp.float32,
    )
    expert_out = summed.astype(jnp.bfloat16)
    full_rows = lax.all_to_all(
        expert_out.reshape(group_size, slots_all, output_column_slice),
        ("dp", "tp"),
        split_axis=0,
        concat_axis=2,
        tiled=True,
    )
    returned = lax.all_to_all(
        full_rows.reshape(ranks_ep, capacity, width), "ep", split_axis=0, concat_axis=0, tiled=True
    )
    returned_rows = returned.reshape(slots_all, width)
    mixed = jnp.zeros((token_rows, width), jnp.float32)
    for route in range(top_routes):
        chosen_rows = jnp.dot(
            places[:, route].astype(jnp.bfloat16), returned_rows, preferred_element_type=jnp.float32
        )
        mixed = mixed + gates[:, route : route + 1] * chosen_rows
    return (attn_out, mixed.astype(jnp.bfloat16))


MESH = pl.DeviceIdType.MESH
PLANE = 8
LAYERS = 4


def window_kernel(
    tables_ref,
    lengths_ref,
    mig_dst_ref,
    mig_seq_ref,
    queries_ref,
    cache_ref,
    pages_ref,
    tokens_ref,
    routes_ref,
    gates_ref,
    gate_w_ref,
    up_w_ref,
    down_w_ref,
    attn_ref,
    moe_ref,
    tok,
    hid,
    out,
    ret,
    wg,
    wu,
    wd,
    qry,
    pool,
    moved,
    part,
    part_in,
    stat,
    stat_in,
    loc_sem,
    zs,
    zr,
    ts,
    tr,
    hs,
    hr,
    os_,
    or_,
    qs,
    qr,
    ms,
    ps,
    pr,
    ss,
    sr,
):
    x = lax.axis_index("dp")
    t = lax.axis_index("tp")
    z = lax.axis_index("ep")
    y = lax.div(t, 2)
    c = lax.rem(t, 2)
    me = x * 4 + t
    ax, ay = lax.rem(x + 1 + c, 2), lax.rem(y + c, 2)
    bx, by = lax.rem(x + c, 2), lax.rem(y + 1 + c, 2)
    at, bt, st = ay * 2 + c, by * 2 + c, y * 2 + (1 - c)
    dev_a, dev_b, dev_s = (ax, at, z), (bx, bt, z), (x, st, z)
    dt = (1 - y) * 2 + c
    id_a, id_b, id_d = ax * 4 + at, bx * 4 + bt, (1 - x) * 4 + dt
    flip = 1 - 2 * c
    z_pair = lax.div(z, 2) * 2 + lax.rem(z + 1, 2)
    inner = lax.div(z + 1, 2) == 1
    outer = lax.rem(lax.div(z + 1, 2), 2) == 0

    half = lax.div(z, 2)

    def layer(i):
        first, last = lax.div(3 - i, 3), lax.div(i, 3)
        middle = 1 - first - last
        other = (2 - i) * (2 - half) + (i - 1) * (3 - 3 * half)
        return first * z + middle * other + last * z_pair

    def remote(src, dst, send, recv, device):
        return pltpu.make_async_remote_copy(
            src_ref=src,
            dst_ref=dst,
            send_sem=send,
            recv_sem=recv,
            device_id=device,
            device_id_type=MESH,
        )

    barrier = pltpu.get_barrier_semaphore()
    world = PLANE * LAYERS

    def greet(j, carry):
        number = lax.rem(me * LAYERS + z + j, world)
        pl.semaphore_signal(
            barrier,
            inc=1,
            device_id=(
                lax.div(number, 16),
                lax.rem(lax.div(number, LAYERS), 4),
                lax.rem(number, LAYERS),
            ),
            device_id_type=MESH,
        )
        return carry

    own_block = tok.at[z, me]
    local = [
        pltpu.make_async_copy(tokens_ref, own_block, loc_sem.at[0]),
        pltpu.make_async_copy(queries_ref, qry.at[t], loc_sem.at[1]),
        pltpu.make_async_copy(cache_ref, pool, loc_sem.at[2]),
        pltpu.make_async_copy(gate_w_ref.at[0], wg, loc_sem.at[3]),
        pltpu.make_async_copy(up_w_ref.at[0], wu, loc_sem.at[4]),
        pltpu.make_async_copy(down_w_ref.at[0], wd, loc_sem.at[5]),
    ]
    for copy in local:
        copy.start()
    lax.fori_loop(1, world, greet, 0)
    pl.semaphore_wait(barrier, world - 1)

    def to_a(buf, k, send, recv):
        return remote(buf.at[k, me], buf.at[k, me], send.at[k, 0], recv.at[k, 0], dev_a)

    def to_b(buf, k, send, recv):
        return remote(buf.at[k, me], buf.at[k, me], send.at[k, 1], recv.at[k, 1], dev_b)

    def on_b(buf, k, send, recv):
        return remote(buf.at[k, id_a], buf.at[k, id_a], send.at[k, 2], recv.at[k, 2], dev_b)

    def to_s(buf, k, send, recv, n, ident):
        return remote(
            buf.at[k, ident], buf.at[k, ident], send.at[k, 3 + n], recv.at[k, 3 + n], dev_s
        )

    def from_s(buf, k, send, recv, n, ident):
        other = ident + flip
        return remote(
            buf.at[k, other], buf.at[k, other], send.at[k, 3 + n], recv.at[k, 3 + n], dev_s
        )

    def arrived(buf, k, send, recv, n, ident):
        return remote(buf.at[k, ident], buf.at[k, ident], send.at[k, n], recv.at[k, n], dev_a)

    def cast_start(*group, plane=True):
        @pl.when(plane)
        def _():
            to_a(*group).start()
            to_b(*group).start()

        to_s(*group, 0, me).start()

    def cast_forward(*group, plane=True):
        arrived(*group, 0, id_a).wait_recv()

        @pl.when(plane)
        def _():
            on_b(*group).start()

        to_s(*group, 1, id_a).start()
        arrived(*group, 1, id_b).wait_recv()
        to_s(*group, 2, id_b).start()

    def cast_end(*group):
        arrived(*group, 2, id_d).wait_recv()
        to_s(*group, 3, id_d).start()
        for n, ident in enumerate((me, id_b, id_a, id_d)):
            from_s(*group, n, ident).wait_recv()

    def cast_sent(*group):
        to_a(*group).wait_send()
        to_b(*group).wait_send()
        on_b(*group).wait_send()
        for n, ident in enumerate((me, id_a, id_b, id_d)):
            to_s(*group, n, ident).wait_send()

    def tok_group(i):
        return (tok, layer(i), ts, tr)

    def hid_group(i):
        return (hid, layer(i), hs, hr)

    def z_copy(k, n, target):
        return remote(tok.at[k, me], tok.at[k, me], zs.at[k, n], zr.at[k], (x, t, target))

    def pair_copy(n, ident):
        return remote(
            tok.at[z, ident], tok.at[z, ident], ts.at[z_pair, n], tr.at[z, n], (x, t, z_pair)
        )

    def out_copy(k, p):
        return remote(
            out.at[k, p],
            ret.at[z, me],
            os_.at[k, p],
            or_.at[z, me],
            (lax.div(p, 4), lax.rem(p, 4), k),
        )

    def out_send(i):
        k = layer(i)

        def send(j, carry):
            out_copy(k, lax.rem(me + j, PLANE)).start()
            return carry

        lax.fori_loop(lax.div(3 - i, 3), PLANE, send, 0)

    local[0].wait()
    z_copy(z, 0, z_pair).start()

    @pl.when(inner)
    def _():
        z_copy(z, 1, 3 - z).start()

    y_dev, x_dev = (x, dt, z), (1 - x, t, z)
    local[1].wait()
    q_far = remote(qry.at[t], qry.at[t], qs.at[0], qr.at[0], y_dev)
    q_near = remote(qry.at[t], qry.at[t], qs.at[1], qr.at[1], dev_s)
    q_far.start()
    q_near.start()
    page_copy = remote(pages_ref, moved, ms.at[0], ms.at[1], x_dev)
    q_pass = remote(qry.at[dt], qry.at[dt], qs.at[2], qr.at[2], dev_s)
    sd = (1 - y) * 2 + (1 - c)

    def part_copies(n):
        u = (st, sd, dt)[n]
        device = (dev_s, dev_s, y_dev)[n]
        return (
            remote(part.at[u], part_in.at[n], ps.at[n], pr.at[n], device),
            remote(stat.at[u], stat_in.at[n], ss.at[n], sr.at[n], device),
        )

    def merge(mine, slots):
        tops = [stat[mine, :, 0:3]] + [stat_in[n, :, 0:3] for n in slots]
        sums = [stat[mine, :, 3:6]] + [stat_in[n, :, 3:6] for n in slots]
        most = functools.reduce(jnp.maximum, tops)
        factors = [jnp.exp(top - most) for top in tops]
        denominator = sum(f * a for f, a in zip(factors, sums))
        numerators = []
        for s in range(3):
            value = factors[0][:, s : s + 1] * part[mine, s].astype(jnp.float32)
            for factor, n in zip(factors[1:], slots):
                value = value + factor[:, s : s + 1] * part_in[n, s].astype(jnp.float32)
            numerators.append(value)
        return most, denominator, numerators

    def pass_on():
        for copy in part_copies(1):
            copy.wait_recv()
        most, denominator, numerators = merge(dt, (1,))
        stat[dt, :, 0:3] = most
        stat[dt, :, 3:6] = denominator
        for s in range(3):
            part[dt, s] = numerators[s].astype(jnp.bfloat16)
        for copy in part_copies(2):
            copy.start()

    def attend():
        remote(qry.at[st], qry.at[st], qs.at[1], qr.at[1], dev_s).wait_recv()
        remote(qry.at[sd], qry.at[sd], qs.at[2], qr.at[2], dev_s).wait_recv()
        local[2].wait()
        page_copy.wait_recv()
        receives = mig_dst_ref[0] == x
        lane = lax.broadcasted_iota(jnp.int32, (HEADS_ALL, 128), 1)
        stats = jnp.zeros((HEADS_ALL, 128), jnp.float32)
        for s in range(3):
            chosen = receives & (mig_seq_ref[0] == s)
            query = qry[:, s].reshape(HEADS_ALL, KV_RANK + ROPE_DIM)
            pages, masked = [], []
            for j in range(SLOTS):
                page = jnp.where(chosen, moved[j], pool[tables_ref[0, s * SLOTS + j]])
                score = (
                    lax.dot_general(
                        query, page, (((1,), (0,)), ((), ())), preferred_element_type=jnp.float32
                    )
                    * score_scale
                )
                position = (j * 4 + t) * PAGE + lax.broadcasted_iota(
                    jnp.int32, (HEADS_ALL, PAGE), 1
                )
                valid = position < lengths_ref[0, 0, s]
                pages.append((page, valid))
                masked.append(jnp.where(valid, score, neg_fill))
            top = jnp.max(jnp.maximum(masked[0], masked[1]), axis=1, keepdims=True)
            total = jnp.zeros((HEADS_ALL, 1), jnp.float32)
            acc = jnp.zeros((HEADS_ALL, KV_RANK), jnp.float32)
            for j in range(SLOTS):
                page, valid = pages[j]
                weight = jnp.where(valid, jnp.exp(masked[j] - top), 0.0).astype(jnp.bfloat16)
                total = total + jnp.sum(weight.astype(jnp.float32), axis=1, keepdims=True)
                acc = acc + lax.dot_general(
                    weight,
                    page[:KV_RANK],
                    (((1,), (1,)), ((), ())),
                    preferred_element_type=jnp.float32,
                )
            stats = jnp.where(lane == s, top, stats)
            stats = jnp.where(lane == 3 + s, total, stats)
            part[:, s] = acc.astype(jnp.bfloat16).reshape(4, HEADS_ALL // 4, KV_RANK)
        stat[...] = stats.reshape(4, HEADS_ALL // 4, 128)
        for n in (1, 0):
            for copy in part_copies(n):
                copy.start()

    def step(i, carry):
        @pl.when(i == 0)
        def _():
            cast_start(*tok_group(0))

        @pl.when((i > 0) & (i < 4))
        def _():
            k = layer(i)

            @pl.when((i < 3) & inner)
            def _():
                z_copy(k, 0, z_pair).wait_recv()
                z_copy(k, 0, z_pair).start()

            @pl.when(i == 1)
            def _():
                @pl.when(inner)
                def _():
                    z_copy(z_pair, 0, z_pair).wait_recv()
                    z_copy(z_pair, 0, 3 - z).start()

                cast_forward(*tok_group(0))

            @pl.when(outer & (i > 0))
            def _():
                z_copy(k, 0, z_pair).wait_recv()

            cast_start(*tok_group(i), plane=i < 3)

        @pl.when((i > 1) & (i < 5))
        def _():
            cast_forward(*tok_group(i - 1), plane=i < 4)

        @pl.when(i == 1)
        def _():
            remote(qry.at[dt], qry.at[dt], qs.at[0], qr.at[0], y_dev).wait_recv()
            q_pass.start()

        @pl.when(i == 3)
        def _():
            page_copy.start()

        @pl.when(i == 2)
        def _():
            local[3].wait()
            local[4].wait()
            local[5].wait()

        @pl.when((i > 1) & (i < 6))
        def _():
            cast_end(*tok_group(i - 2))

            @pl.when(i == 2)
            def _():
                for n, ident in enumerate((id_a, id_b, id_d)):
                    pair_copy(n, ident).start()

            k = layer(i - 2)
            rows = tok[k].reshape(PLANE * 16, tok.shape[3])
            gate = jnp.dot(rows, wg[...], preferred_element_type=jnp.float32)
            up = jnp.dot(rows, wu[...], preferred_element_type=jnp.float32)
            hid[k, me] = (gate / (1.0 + jnp.exp(-gate)) * up).astype(jnp.bfloat16)
            cast_start(*hid_group(i - 2))

        @pl.when(i == 6)
        def _():
            attend()

        @pl.when(i == 7)
        def _():
            pass_on()

        @pl.when((i > 2) & (i < 7))
        def _():
            cast_forward(*hid_group(i - 3))

        @pl.when(i > 3)
        def _():
            cast_end(*hid_group(i - 4))
            k = layer(i - 4)
            depth = hid.shape[3]
            total = jnp.zeros((PLANE * 16, out.shape[3]), jnp.float32)
            for p in range(PLANE):
                total = total + lax.dot_general(
                    hid[k, p],
                    wd[:, p * depth : (p + 1) * depth],
                    (((1,), (1,)), ((), ())),
                    preferred_element_type=jnp.float32,
                )
            out[k] = total.astype(jnp.bfloat16).reshape(PLANE, 16, out.shape[3])
            out_send(i - 4)

        return carry

    lax.fori_loop(0, 8, step, 0)
    keep = pltpu.make_async_copy(out.at[z, me], ret.at[z, me], loc_sem.at[6])
    keep.start()

    for n in (0, 2):
        for copy in part_copies(n):
            copy.wait_recv()
    most, denominator, numerators = merge(t, (0, 2))
    for s in range(3):
        attn_ref[s] = (numerators[s] / denominator[:, s : s + 1]).astype(jnp.bfloat16)

    q_far.wait_send()
    q_near.wait_send()
    q_pass.wait_send()
    page_copy.wait_send()
    for n in range(3):
        for copy in part_copies(n):
            copy.wait_send()
    z_copy(z, 0, z_pair).wait_send()

    @pl.when(inner)
    def _():
        z_copy(z, 1, 3 - z).wait_send()

    def drain(i, carry):
        @pl.when((i > 0) & inner)
        def _():
            z_copy(layer(i), 0, z_pair).wait_send()

        cast_sent(*tok_group(i))
        cast_sent(*hid_group(i))
        return carry

    lax.fori_loop(0, 4, drain, 0)

    def out_wait(i, carry):
        k = layer(i)

        def one(j, inside):
            p = lax.rem(me + j, PLANE)
            out_copy(k, p).wait_send()
            remote(out.at[k, p], ret.at[k, p], os_.at[k, p], or_.at[k, p], dev_s).wait_recv()
            return inside

        return lax.fori_loop(lax.div(3 - i, 3), PLANE, one, carry)

    lax.fori_loop(0, 4, out_wait, 0)
    keep.wait()
    named, scale = routes_ref[...], gates_ref[...]
    count = named.shape[1]
    same = lax.broadcasted_iota(jnp.int32, (count, count), 0) == lax.broadcasted_iota(
        jnp.int32, (count, count), 1
    )
    coefs = []
    for e in range(LAYERS):
        hits = jnp.sum(jnp.where(named == e, scale, 0.0), axis=0, keepdims=True)
        coefs.append(jnp.sum(jnp.where(same, hits, 0.0), axis=1, keepdims=True))
    span = out.shape[3]
    for p in range(PLANE):
        mixed = coefs[0] * ret[0, p].astype(jnp.float32)
        for e in range(1, LAYERS):
            mixed = mixed + coefs[e] * ret[e, p].astype(jnp.float32)
        moe_ref[:, p * span : (p + 1) * span] = mixed.astype(jnp.bfloat16)


HEADS_ALL = 128


def window(
    queries,
    cache,
    tables,
    lengths,
    mig_cache,
    mig_src,
    mig_dst,
    mig_seq,
    tokens,
    routes,
    gates,
    gate_w,
    up_w,
    down_w,
):
    rows, width = tokens.shape
    depth, span, units = gate_w.shape[2], down_w.shape[2], down_w.shape[1]
    heads, row_width = queries.shape[1], queries.shape[2]
    pool, moved = jnp.swapaxes(cache, 1, 2), jnp.swapaxes(mig_cache, 1, 2)
    bf16, f32 = jnp.bfloat16, jnp.float32
    dma = pltpu.SemaphoreType.DMA
    smem = pl.BlockSpec(memory_space=pltpu.SMEM)
    vmem = pl.BlockSpec(memory_space=pltpu.VMEM)
    hbm = pl.BlockSpec(memory_space=pltpu.HBM)
    return pl.pallas_call(
        window_kernel,
        out_shape=(
            jax.ShapeDtypeStruct((queries.shape[0], heads, KV_RANK), bf16),
            jax.ShapeDtypeStruct((rows, width), bf16),
        ),
        in_specs=[smem] * 4 + [hbm] * 4 + [vmem] * 2 + [hbm] * 3,
        out_specs=(vmem, vmem),
        scratch_shapes=[
            pltpu.VMEM((LAYERS, PLANE, rows, width), bf16),
            pltpu.VMEM((LAYERS, PLANE, PLANE * rows, depth), bf16),
            pltpu.VMEM((LAYERS, PLANE, rows, span), bf16),
            pltpu.VMEM((LAYERS, PLANE, rows, span), bf16),
            pltpu.VMEM((width, depth), bf16),
            pltpu.VMEM((width, depth), bf16),
            pltpu.VMEM((span, units), bf16),
            pltpu.VMEM((4, 3, heads, row_width), bf16),
            pltpu.VMEM(pool.shape, bf16),
            pltpu.VMEM(moved.shape, bf16),
            pltpu.VMEM((4, 3, heads, KV_RANK), bf16),
            pltpu.VMEM((3, 3, heads, KV_RANK), bf16),
            pltpu.VMEM((4, heads, 128), f32),
            pltpu.VMEM((3, heads, 128), f32),
            dma((7,)),
            dma((4, 2)),
            dma((4,)),
            dma((4, 7)),
            dma((4, 7)),
            dma((4, 7)),
            dma((4, 7)),
            dma((4, PLANE)),
            dma((4, PLANE)),
            dma((3,)),
            dma((3,)),
            dma((2,)),
            dma((3,)),
            dma((3,)),
            dma((3,)),
            dma((3,)),
        ],
        compiler_params=pltpu.CompilerParams(
            collective_id=0, has_side_effects=True, vmem_limit_bytes=40 * 1024 * 1024
        ),
    )(
        tables,
        lengths,
        mig_dst,
        mig_seq,
        queries,
        pool,
        moved,
        tokens,
        routes.T,
        gates.T,
        gate_w,
        up_w,
        jnp.swapaxes(down_w, 1, 2),
    )


def solution(mesh):
    form = per_device
    if (mesh.shape["dp"], mesh.shape["tp"], mesh.shape["ep"]) == (2, 4, LAYERS):
        form = window
    in_specs = (
        P(("dp", "ep"), "tp", None),
        P(("dp", "tp", "ep"), None, None),
        P(("dp", "tp", "ep"), None),
        P("dp", "ep", None),
        P(("dp", "tp", "ep"), None, None),
        P("ep"),
        P("ep"),
        P("ep"),
        P(("dp", "tp", "ep"), None),
        P(("dp", "tp", "ep"), None),
        P(("dp", "tp", "ep"), None),
        P("ep", None, ("dp", "tp")),
        P("ep", None, ("dp", "tp")),
        P("ep", None, ("dp", "tp")),
    )
    out_specs = (P(("dp", "ep"), "tp", None), P(("dp", "tp", "ep"), None))
    return jax.shard_map(
        form, mesh=mesh, in_specs=in_specs, out_specs=out_specs, check_vma=False
    )
```

```python
import functools

import jax
import jax.numpy as jnp
from jax import lax
from jax.experimental import pallas as pl
from jax.experimental.pallas import tpu as pltpu
from jax.sharding import PartitionSpec as P

KV_RANK = 512
ROPE_DIM = 64
PAGE = 128
SLOTS = 2


score_scale = 0.07216878364870322
neg_fill = -1e30


def broadcast(x, axis, root):
    mine = lax.axis_index(axis) == root
    return lax.psum(jnp.where(mine, x, jnp.zeros_like(x)), axis)


def per_device(
    queries,
    cache,
    tables,
    lengths,
    mig_cache,
    mig_src,
    mig_dst,
    mig_seq,
    tokens,
    routes,
    gates,
    gate_w,
    up_w,
    down_w,
):
    tensor_parallel_ranks = lax.axis_size("tp")
    rank_tp = lax.axis_index("tp")
    rank_dp = lax.axis_index("dp")
    row_width = KV_RANK + ROPE_DIM
    group_query = lax.all_gather(queries, "tp", axis=1, tiled=True)
    seqs_group = group_query.shape[0]
    moved_pages = broadcast(mig_cache, "dp", mig_src[0])
    own_pages = cache[tables.reshape(seqs_group, SLOTS)]
    chosen = (rank_dp == mig_dst[0]) & (jnp.arange(seqs_group) == mig_seq[0])
    key_rows = jnp.where(chosen[:, None, None, None], moved_pages[None], own_pages)
    key_rows = key_rows.reshape(seqs_group, SLOTS * PAGE, row_width)
    positions = (
        (jnp.arange(SLOTS)[:, None] * tensor_parallel_ranks + rank_tp) * PAGE
        + jnp.arange(PAGE)[None, :]
    ).reshape(-1)
    valid = positions[None, :] < lengths[0, 0][:, None]
    scores = (
        jnp.einsum("shc,skc->shk", group_query, key_rows, preferred_element_type=jnp.float32)
        * score_scale
    )
    masked = jnp.where(valid[:, None, :], scores, neg_fill)
    part_max = jnp.max(masked, axis=2)
    weights = jnp.where(valid[:, None, :], jnp.exp(masked - part_max[..., None]), 0.0).astype(
        jnp.bfloat16
    )
    part_sum = jnp.sum(weights.astype(jnp.float32), axis=2)
    part_acc = jnp.einsum(
        "shk,skc->shc", weights, key_rows[:, :, :KV_RANK], preferred_element_type=jnp.float32
    )
    most = lax.pmax(part_max, "tp")
    factor = jnp.exp(part_max - most)
    numerator, denominator = (
        lax.psum_scatter(part_acc * factor[..., None], "tp", scatter_dimension=1, tiled=True),
        lax.psum_scatter(part_sum * factor, "tp", scatter_dimension=1, tiled=True),
    )
    attn_out = (numerator / denominator[..., None]).astype(jnp.bfloat16)
    ranks_ep = lax.axis_size("ep")
    token_rows = tokens.shape[0]
    top_routes = routes.shape[1]
    width = tokens.shape[1]
    capacity = min(token_rows, max(2, 2 * token_rows * top_routes // ranks_ep))
    slots_all = ranks_ep * capacity
    flattened_index_list = routes.reshape(-1)
    matches = (flattened_index_list[:, None] == jnp.arange(ranks_ep)[None, :]).astype(jnp.int32)
    before = jnp.cumsum(matches, axis=0) - matches
    column = flattened_index_list * capacity + jnp.sum(before * matches, axis=1)
    places = (column[:, None] == jnp.arange(slots_all)[None, :]).reshape(
        token_rows, top_routes, slots_all
    )
    selected_entries = jnp.any(places, axis=1).astype(jnp.bfloat16)
    dispatched_rows = lax.dot_general(
        selected_entries, tokens, (((0,), (0,)), ((), ())), preferred_element_type=jnp.float32
    )
    dispatched_rows = dispatched_rows.astype(jnp.bfloat16).reshape(ranks_ep, capacity, width)
    weight_gate = gate_w[0]
    weight_up = up_w[0]
    weight_down = down_w[0]
    arrived = lax.all_to_all(dispatched_rows, "ep", split_axis=0, concat_axis=0, tiled=True)
    piece = lax.all_gather(arrived[None], ("dp", "tp"), axis=0, tiled=True)
    piece_rows = piece.reshape(-1, width)
    gate = jnp.dot(piece_rows, weight_gate, preferred_element_type=jnp.float32)
    upward = jnp.dot(piece_rows, weight_up, preferred_element_type=jnp.float32)
    hidden_piece = (jax.nn.silu(gate) * upward).astype(jnp.bfloat16)
    hidden = hidden_piece.reshape(piece.shape[:-1] + (weight_gate.shape[1],))
    group_size = hidden.shape[0]
    total_rows = group_size * slots_all
    output_column_slice = weight_down.shape[1]
    summed = jnp.dot(
        lax.all_gather(hidden, ("dp", "tp"), axis=3, tiled=True).reshape(total_rows, -1),
        weight_down,
        preferred_element_type=jnp.float32,
    )
    expert_out = summed.astype(jnp.bfloat16)
    full_rows = lax.all_to_all(
        expert_out.reshape(group_size, slots_all, output_column_slice),
        ("dp", "tp"),
        split_axis=0,
        concat_axis=2,
        tiled=True,
    )
    returned = lax.all_to_all(
        full_rows.reshape(ranks_ep, capacity, width), "ep", split_axis=0, concat_axis=0, tiled=True
    )
    returned_rows = returned.reshape(slots_all, width)
    mixed = jnp.zeros((token_rows, width), jnp.float32)
    for route in range(top_routes):
        chosen_rows = jnp.dot(
            places[:, route].astype(jnp.bfloat16), returned_rows, preferred_element_type=jnp.float32
        )
        mixed = mixed + gates[:, route : route + 1] * chosen_rows
    return (attn_out, mixed.astype(jnp.bfloat16))


MESH = pl.DeviceIdType.MESH
PLANE = 8
LAYERS = 4


def window_kernel(
    tables_ref,
    lengths_ref,
    mig_dst_ref,
    mig_seq_ref,
    queries_ref,
    cache_ref,
    pages_ref,
    tokens_ref,
    gate_w_ref,
    up_w_ref,
    down_w_ref,
    attn_ref,
    ret,
    tok,
    hid,
    out,
    wg,
    wu,
    wd,
    qry,
    pool,
    moved,
    part,
    part_in,
    stat,
    stat_in,
    loc_sem,
    zs,
    zr,
    ts,
    tr,
    hs,
    hr,
    os_,
    or_,
    qs,
    qr,
    ms,
    ps,
    pr,
    ss,
    sr,
):
    x = lax.axis_index("dp")
    t = lax.axis_index("tp")
    z = lax.axis_index("ep")
    y = lax.div(t, 2)
    c = lax.rem(t, 2)
    me = x * 4 + t
    ax, ay = lax.rem(x + 1 + c, 2), lax.rem(y + c, 2)
    bx, by = lax.rem(x + c, 2), lax.rem(y + 1 + c, 2)
    at, bt, st = ay * 2 + c, by * 2 + c, y * 2 + (1 - c)
    dev_a, dev_b, dev_s = (ax, at, z), (bx, bt, z), (x, st, z)
    dt = (1 - y) * 2 + c
    id_a, id_b, id_d = ax * 4 + at, bx * 4 + bt, (1 - x) * 4 + dt
    flip = 1 - 2 * c
    z_pair = lax.div(z, 2) * 2 + lax.rem(z + 1, 2)
    inner = lax.div(z + 1, 2) == 1

    half = lax.div(z, 2)

    def layer(i):
        first, last = lax.div(3 - i, 3), lax.div(i, 3)
        middle = 1 - first - last
        other = (2 - i) * (2 - half) + (i - 1) * (3 - 3 * half)
        return first * z + middle * other + last * z_pair

    def remote(src, dst, send, recv, device):
        return pltpu.make_async_remote_copy(
            src_ref=src,
            dst_ref=dst,
            send_sem=send,
            recv_sem=recv,
            device_id=device,
            device_id_type=MESH,
        )

    barrier = pltpu.get_barrier_semaphore()
    world = PLANE * LAYERS

    def greet(j, carry):
        number = lax.rem(me * LAYERS + z + j, world)
        pl.semaphore_signal(
            barrier,
            inc=1,
            device_id=(
                lax.div(number, 16),
                lax.rem(lax.div(number, LAYERS), 4),
                lax.rem(number, LAYERS),
            ),
            device_id_type=MESH,
        )
        return carry

    own_block = tok.at[z, me]
    local = [
        pltpu.make_async_copy(tokens_ref, own_block, loc_sem.at[0]),
        pltpu.make_async_copy(queries_ref, qry.at[t], loc_sem.at[1]),
        pltpu.make_async_copy(cache_ref, pool, loc_sem.at[2]),
        pltpu.make_async_copy(gate_w_ref.at[0], wg, loc_sem.at[3]),
        pltpu.make_async_copy(up_w_ref.at[0], wu, loc_sem.at[4]),
        pltpu.make_async_copy(down_w_ref.at[0], wd, loc_sem.at[5]),
    ]
    for copy in local:
        copy.start()
    lax.fori_loop(1, world, greet, 0)
    pl.semaphore_wait(barrier, world - 1)

    def to_a(buf, k, send, recv):
        return remote(buf.at[k, me], buf.at[k, me], send.at[k, 0], recv.at[k, 0], dev_a)

    def to_b(buf, k, send, recv):
        return remote(buf.at[k, me], buf.at[k, me], send.at[k, 1], recv.at[k, 1], dev_b)

    def on_b(buf, k, send, recv):
        return remote(buf.at[k, id_a], buf.at[k, id_a], send.at[k, 2], recv.at[k, 2], dev_b)

    def to_s(buf, k, send, recv, n, ident):
        return remote(
            buf.at[k, ident], buf.at[k, ident], send.at[k, 3 + n], recv.at[k, 3 + n], dev_s
        )

    def from_s(buf, k, send, recv, n, ident):
        other = ident + flip
        return remote(
            buf.at[k, other], buf.at[k, other], send.at[k, 3 + n], recv.at[k, 3 + n], dev_s
        )

    def arrived(buf, k, send, recv, n, ident):
        return remote(buf.at[k, ident], buf.at[k, ident], send.at[k, n], recv.at[k, n], dev_a)

    def cast_start(*group, plane=True):
        @pl.when(plane)
        def _():
            to_a(*group).start()
            to_b(*group).start()

        to_s(*group, 0, me).start()

    def cast_forward(*group, plane=True):
        arrived(*group, 0, id_a).wait_recv()

        @pl.when(plane)
        def _():
            on_b(*group).start()

        to_s(*group, 1, id_a).start()
        arrived(*group, 1, id_b).wait_recv()
        to_s(*group, 2, id_b).start()

    def cast_end(*group):
        arrived(*group, 2, id_d).wait_recv()
        to_s(*group, 3, id_d).start()
        for n, ident in enumerate((me, id_b, id_a, id_d)):
            from_s(*group, n, ident).wait_recv()

    def cast_sent(*group):
        to_a(*group).wait_send()
        to_b(*group).wait_send()
        on_b(*group).wait_send()
        for n, ident in enumerate((me, id_a, id_b, id_d)):
            to_s(*group, n, ident).wait_send()

    def tok_group(i):
        return (tok, layer(i), ts, tr)

    def hid_group(i):
        return (hid, layer(i), hs, hr)

    def z_copy(k, n, target):
        return remote(tok.at[k, me], tok.at[k, me], zs.at[k, n], zr.at[k], (x, t, target))

    def pair_copy(n, ident):
        return remote(
            tok.at[z, ident], tok.at[z, ident], ts.at[z_pair, n], tr.at[z, n], (x, t, z_pair)
        )

    def out_copy(k, p):
        return remote(
            out.at[k, p],
            ret.at[z, me],
            os_.at[k, p],
            or_.at[z, me],
            (lax.div(p, 4), lax.rem(p, 4), k),
        )

    def out_send(i):
        k = layer(i)

        def send(j, carry):
            out_copy(k, lax.rem(me + j, PLANE)).start()
            return carry

        lax.fori_loop(lax.div(3 - i, 3), PLANE, send, 0)

    local[0].wait()
    z_copy(z, 0, z_pair).start()

    @pl.when(inner)
    def _():
        z_copy(z, 1, 3 - z).start()

    y_dev, x_dev = (x, dt, z), (1 - x, t, z)
    local[1].wait()
    q_far = remote(qry.at[t], qry.at[t], qs.at[0], qr.at[0], y_dev)
    q_near = remote(qry.at[t], qry.at[t], qs.at[1], qr.at[1], dev_s)
    q_far.start()
    q_near.start()
    page_copy = remote(pages_ref, moved, ms.at[0], ms.at[1], x_dev)
    q_pass = remote(qry.at[dt], qry.at[dt], qs.at[2], qr.at[2], dev_s)
    sd = (1 - y) * 2 + (1 - c)

    def part_copies(n):
        u = (st, sd, dt)[n]
        device = (dev_s, dev_s, y_dev)[n]
        return (
            remote(part.at[u], part_in.at[n], ps.at[n], pr.at[n], device),
            remote(stat.at[u], stat_in.at[n], ss.at[n], sr.at[n], device),
        )

    def merge(mine, slots):
        tops = [stat[mine, :, 0:3]] + [stat_in[n, :, 0:3] for n in slots]
        sums = [stat[mine, :, 3:6]] + [stat_in[n, :, 3:6] for n in slots]
        most = functools.reduce(jnp.maximum, tops)
        factors = [jnp.exp(top - most) for top in tops]
        denominator = sum(f * a for f, a in zip(factors, sums))
        numerators = []
        for s in range(3):
            value = factors[0][:, s : s + 1] * part[mine, s].astype(jnp.float32)
            for factor, n in zip(factors[1:], slots):
                value = value + factor[:, s : s + 1] * part_in[n, s].astype(jnp.float32)
            numerators.append(value)
        return most, denominator, numerators

    def pass_on():
        for copy in part_copies(1):
            copy.wait_recv()
        most, denominator, numerators = merge(dt, (1,))
        stat[dt, :, 0:3] = most
        stat[dt, :, 3:6] = denominator
        for s in range(3):
            part[dt, s] = numerators[s].astype(jnp.bfloat16)
        for copy in part_copies(2):
            copy.start()

    def attend():
        remote(qry.at[st], qry.at[st], qs.at[1], qr.at[1], dev_s).wait_recv()
        remote(qry.at[sd], qry.at[sd], qs.at[2], qr.at[2], dev_s).wait_recv()
        local[2].wait()
        page_copy.wait_recv()
        receives = mig_dst_ref[0] == x
        lane = lax.broadcasted_iota(jnp.int32, (HEADS_ALL, 128), 1)
        stats = jnp.zeros((HEADS_ALL, 128), jnp.float32)
        for s in range(3):
            chosen = receives & (mig_seq_ref[0] == s)
            query = qry[:, s].reshape(HEADS_ALL, KV_RANK + ROPE_DIM)
            pages, masked = [], []
            for j in range(SLOTS):
                page = jnp.where(chosen, moved[j], pool[tables_ref[0, s * SLOTS + j]])
                score = (
                    lax.dot_general(
                        query, page, (((1,), (0,)), ((), ())), preferred_element_type=jnp.float32
                    )
                    * score_scale
                )
                position = (j * 4 + t) * PAGE + lax.broadcasted_iota(
                    jnp.int32, (HEADS_ALL, PAGE), 1
                )
                valid = position < lengths_ref[0, 0, s]
                pages.append((page, valid))
                masked.append(jnp.where(valid, score, neg_fill))
            top = jnp.max(jnp.maximum(masked[0], masked[1]), axis=1, keepdims=True)
            total = jnp.zeros((HEADS_ALL, 1), jnp.float32)
            acc = jnp.zeros((HEADS_ALL, KV_RANK), jnp.float32)
            for j in range(SLOTS):
                page, valid = pages[j]
                weight = jnp.where(valid, jnp.exp(masked[j] - top), 0.0).astype(jnp.bfloat16)
                total = total + jnp.sum(weight.astype(jnp.float32), axis=1, keepdims=True)
                acc = acc + lax.dot_general(
                    weight,
                    page[:KV_RANK],
                    (((1,), (1,)), ((), ())),
                    preferred_element_type=jnp.float32,
                )
            stats = jnp.where(lane == s, top, stats)
            stats = jnp.where(lane == 3 + s, total, stats)
            part[:, s] = acc.astype(jnp.bfloat16).reshape(4, HEADS_ALL // 4, KV_RANK)
        stat[...] = stats.reshape(4, HEADS_ALL // 4, 128)
        for n in (1, 0):
            for copy in part_copies(n):
                copy.start()

    def step(i, carry):
        @pl.when(i == 0)
        def _():
            cast_start(*tok_group(0))

        @pl.when((i > 0) & (i < 4))
        def _():
            k = layer(i)

            @pl.when(i < 3)
            def _():
                z_copy(k, 0, z_pair).wait_recv()

                @pl.when(inner)
                def _():
                    z_copy(k, 0, z_pair).start()

            @pl.when(i == 1)
            def _():
                z_copy(z_pair, 0, z_pair).wait_recv()

                @pl.when(inner)
                def _():
                    z_copy(z_pair, 0, 3 - z).start()

            cast_start(*tok_group(i), plane=i < 3)

        @pl.when((i > 0) & (i < 5))
        def _():
            cast_forward(*tok_group(i - 1), plane=i < 4)

        @pl.when(i == 1)
        def _():
            remote(qry.at[dt], qry.at[dt], qs.at[0], qr.at[0], y_dev).wait_recv()
            q_pass.start()

        @pl.when(i == 2)
        def _():
            page_copy.start()
            local[3].wait()
            local[4].wait()
            local[5].wait()

        @pl.when(i == 5)
        def _():
            attend()

        @pl.when((i > 1) & (i < 6))
        def _():
            cast_end(*tok_group(i - 2))

            @pl.when(i == 2)
            def _():
                for n, ident in enumerate((id_a, id_b, id_d)):
                    pair_copy(n, ident).start()

            k = layer(i - 2)
            rows = tok[k].reshape(PLANE * 16, tok.shape[3])
            gate = jnp.dot(rows, wg[...], preferred_element_type=jnp.float32)
            up = jnp.dot(rows, wu[...], preferred_element_type=jnp.float32)
            hid[k, me] = (gate / (1.0 + jnp.exp(-gate)) * up).astype(jnp.bfloat16)
            cast_start(*hid_group(i - 2))

        @pl.when(i == 6)
        def _():
            pass_on()

        @pl.when((i > 2) & (i < 7))
        def _():
            cast_forward(*hid_group(i - 3))

        @pl.when(i > 3)
        def _():
            cast_end(*hid_group(i - 4))
            k = layer(i - 4)
            depth = hid.shape[3]
            total = jnp.zeros((PLANE * 16, out.shape[3]), jnp.float32)
            for p in range(PLANE):
                total = total + lax.dot_general(
                    hid[k, p],
                    wd[:, p * depth : (p + 1) * depth],
                    (((1,), (1,)), ((), ())),
                    preferred_element_type=jnp.float32,
                )
            out[k] = total.astype(jnp.bfloat16).reshape(PLANE, 16, out.shape[3])
            out_send(i - 4)

        return carry

    lax.fori_loop(0, 8, step, 0)
    keep = pltpu.make_async_copy(out.at[z, me], ret.at[z, me], loc_sem.at[6])
    keep.start()

    for n in (0, 2):
        for copy in part_copies(n):
            copy.wait_recv()
    most, denominator, numerators = merge(t, (0, 2))
    for s in range(3):
        attn_ref[s] = (numerators[s] / denominator[:, s : s + 1]).astype(jnp.bfloat16)

    q_far.wait_send()
    q_near.wait_send()
    q_pass.wait_send()
    page_copy.wait_send()
    for n in range(3):
        for copy in part_copies(n):
            copy.wait_send()
    z_copy(z, 0, z_pair).wait_send()

    @pl.when(inner)
    def _():
        z_copy(z, 1, 3 - z).wait_send()

    def drain(i, carry):
        @pl.when((i > 0) & inner)
        def _():
            z_copy(layer(i), 0, z_pair).wait_send()

        cast_sent(*tok_group(i))
        cast_sent(*hid_group(i))
        return carry

    lax.fori_loop(0, 4, drain, 0)

    def out_wait(i, carry):
        k = layer(i)

        def one(j, inside):
            p = lax.rem(me + j, PLANE)
            out_copy(k, p).wait_send()
            remote(out.at[k, p], ret.at[k, p], os_.at[k, p], or_.at[k, p], dev_s).wait_recv()
            return inside

        return lax.fori_loop(lax.div(3 - i, 3), PLANE, one, carry)

    lax.fori_loop(0, 4, out_wait, 0)
    keep.wait()


def mix_kernel(raw_ref, ret, routes_ref, gates_ref, attn_ref, moe_ref):
    attn_ref[...] = raw_ref[...]
    named, scale = routes_ref[...], gates_ref[...]
    count = named.shape[1]
    same = lax.broadcasted_iota(jnp.int32, (count, count), 0) == lax.broadcasted_iota(
        jnp.int32, (count, count), 1
    )
    coefs = []
    for e in range(LAYERS):
        hits = jnp.sum(jnp.where(named == e, scale, 0.0), axis=0, keepdims=True)
        coefs.append(jnp.sum(jnp.where(same, hits, 0.0), axis=1, keepdims=True))
    span = ret.shape[3]
    for p in range(PLANE):
        mixed = coefs[0] * ret[0, p].astype(jnp.float32)
        for e in range(1, LAYERS):
            mixed = mixed + coefs[e] * ret[e, p].astype(jnp.float32)
        moe_ref[:, p * span : (p + 1) * span] = mixed.astype(jnp.bfloat16)


HEADS_ALL = 128


def window(
    queries,
    cache,
    tables,
    lengths,
    mig_cache,
    mig_src,
    mig_dst,
    mig_seq,
    tokens,
    routes,
    gates,
    gate_w,
    up_w,
    down_w,
):
    rows, width = tokens.shape
    depth, span, units = gate_w.shape[2], down_w.shape[2], down_w.shape[1]
    heads, row_width = queries.shape[1], queries.shape[2]
    pool, moved = jnp.swapaxes(cache, 1, 2), jnp.swapaxes(mig_cache, 1, 2)
    bf16, f32 = jnp.bfloat16, jnp.float32
    dma = pltpu.SemaphoreType.DMA
    smem = pl.BlockSpec(memory_space=pltpu.SMEM)
    vmem = pl.BlockSpec(memory_space=pltpu.VMEM)
    hbm = pl.BlockSpec(memory_space=pl.ANY)
    raw, returned = pl.pallas_call(
        window_kernel,
        out_shape=(
            jax.ShapeDtypeStruct((queries.shape[0], heads, KV_RANK), bf16),
            jax.ShapeDtypeStruct((LAYERS, PLANE, rows, span), bf16),
        ),
        in_specs=[smem] * 4 + [hbm] * 7,
        out_specs=(vmem, hbm),
        scratch_shapes=[
            pltpu.VMEM((LAYERS, PLANE, rows, width), bf16),
            pltpu.VMEM((LAYERS, PLANE, PLANE * rows, depth), bf16),
            pltpu.VMEM((LAYERS, PLANE, rows, span), bf16),
            pltpu.VMEM((width, depth), bf16),
            pltpu.VMEM((width, depth), bf16),
            pltpu.VMEM((span, units), bf16),
            pltpu.VMEM((4, 3, heads, row_width), bf16),
            pltpu.VMEM(pool.shape, bf16),
            pltpu.VMEM(moved.shape, bf16),
            pltpu.VMEM((4, 3, heads, KV_RANK), bf16),
            pltpu.VMEM((3, 3, heads, KV_RANK), bf16),
            pltpu.VMEM((4, heads, 128), f32),
            pltpu.VMEM((3, heads, 128), f32),
            dma((7,)),
            dma((4, 2)),
            dma((4,)),
            dma((4, 7)),
            dma((4, 7)),
            dma((4, 7)),
            dma((4, 7)),
            dma((4, PLANE)),
            dma((4, PLANE)),
            dma((3,)),
            dma((3,)),
            dma((2,)),
            dma((3,)),
            dma((3,)),
            dma((3,)),
            dma((3,)),
        ],
        compiler_params=pltpu.CompilerParams(
            collective_id=0, has_side_effects=True, vmem_limit_bytes=60 * 1024 * 1024
        ),
    )(
        tables,
        lengths,
        mig_dst,
        mig_seq,
        queries,
        pool,
        moved,
        tokens,
        gate_w,
        up_w,
        jnp.swapaxes(down_w, 1, 2),
    )
    return pl.pallas_call(
        mix_kernel,
        out_shape=(
            jax.ShapeDtypeStruct(raw.shape, bf16),
            jax.ShapeDtypeStruct((rows, width), bf16),
        ),
        in_specs=[vmem] * 4,
        out_specs=(vmem, vmem),
        compiler_params=pltpu.CompilerParams(vmem_limit_bytes=60 * 1024 * 1024),
    )(raw, returned, routes.T, gates.T)


def solution(mesh):
    form = per_device
    if (mesh.shape["dp"], mesh.shape["tp"], mesh.shape["ep"]) == (2, 4, LAYERS):
        form = window
    in_specs = (
        P(("dp", "ep"), "tp", None),
        P(("dp", "tp", "ep"), None, None),
        P(("dp", "tp", "ep"), None),
        P("dp", "ep", None),
        P(("dp", "tp", "ep"), None, None),
        P("ep"),
        P("ep"),
        P("ep"),
        P(("dp", "tp", "ep"), None),
        P(("dp", "tp", "ep"), None),
        P(("dp", "tp", "ep"), None),
        P("ep", None, ("dp", "tp")),
        P("ep", None, ("dp", "tp")),
        P("ep", None, ("dp", "tp")),
    )
    out_specs = (P(("dp", "ep"), "tp", None), P(("dp", "tp", "ep"), None))
    return jax.shard_map(
        form, mesh=mesh, in_specs=in_specs, out_specs=out_specs, check_vma=False
    )
```

```python
import functools

import jax
import jax.numpy as jnp
from jax import lax
from jax.experimental import pallas as pl
from jax.experimental.pallas import tpu as pltpu
from jax.sharding import PartitionSpec as P

KV_RANK = 512
ROPE_DIM = 64
PAGE = 128
SLOTS = 2


score_scale = 0.07216878364870322
neg_fill = -1e30


def broadcast(x, axis, root):
    mine = lax.axis_index(axis) == root
    return lax.psum(jnp.where(mine, x, jnp.zeros_like(x)), axis)


def per_device(
    queries,
    cache,
    tables,
    lengths,
    mig_cache,
    mig_src,
    mig_dst,
    mig_seq,
    tokens,
    routes,
    gates,
    gate_w,
    up_w,
    down_w,
):
    tensor_parallel_ranks = lax.axis_size("tp")
    rank_tp = lax.axis_index("tp")
    rank_dp = lax.axis_index("dp")
    row_width = KV_RANK + ROPE_DIM
    group_query = lax.all_gather(queries, "tp", axis=1, tiled=True)
    seqs_group = group_query.shape[0]
    moved_pages = broadcast(mig_cache, "dp", mig_src[0])
    own_pages = cache[tables.reshape(seqs_group, SLOTS)]
    chosen = (rank_dp == mig_dst[0]) & (jnp.arange(seqs_group) == mig_seq[0])
    key_rows = jnp.where(chosen[:, None, None, None], moved_pages[None], own_pages)
    key_rows = key_rows.reshape(seqs_group, SLOTS * PAGE, row_width)
    positions = (
        (jnp.arange(SLOTS)[:, None] * tensor_parallel_ranks + rank_tp) * PAGE
        + jnp.arange(PAGE)[None, :]
    ).reshape(-1)
    valid = positions[None, :] < lengths[0, 0][:, None]
    scores = (
        jnp.einsum("shc,skc->shk", group_query, key_rows, preferred_element_type=jnp.float32)
        * score_scale
    )
    masked = jnp.where(valid[:, None, :], scores, neg_fill)
    part_max = jnp.max(masked, axis=2)
    weights = jnp.where(valid[:, None, :], jnp.exp(masked - part_max[..., None]), 0.0).astype(
        jnp.bfloat16
    )
    part_sum = jnp.sum(weights.astype(jnp.float32), axis=2)
    part_acc = jnp.einsum(
        "shk,skc->shc", weights, key_rows[:, :, :KV_RANK], preferred_element_type=jnp.float32
    )
    most = lax.pmax(part_max, "tp")
    factor = jnp.exp(part_max - most)
    numerator, denominator = (
        lax.psum_scatter(part_acc * factor[..., None], "tp", scatter_dimension=1, tiled=True),
        lax.psum_scatter(part_sum * factor, "tp", scatter_dimension=1, tiled=True),
    )
    attn_out = (numerator / denominator[..., None]).astype(jnp.bfloat16)
    ranks_ep = lax.axis_size("ep")
    token_rows = tokens.shape[0]
    top_routes = routes.shape[1]
    width = tokens.shape[1]
    capacity = min(token_rows, max(2, 2 * token_rows * top_routes // ranks_ep))
    slots_all = ranks_ep * capacity
    flattened_index_list = routes.reshape(-1)
    matches = (flattened_index_list[:, None] == jnp.arange(ranks_ep)[None, :]).astype(jnp.int32)
    before = jnp.cumsum(matches, axis=0) - matches
    column = flattened_index_list * capacity + jnp.sum(before * matches, axis=1)
    places = (column[:, None] == jnp.arange(slots_all)[None, :]).reshape(
        token_rows, top_routes, slots_all
    )
    selected_entries = jnp.any(places, axis=1).astype(jnp.bfloat16)
    dispatched_rows = lax.dot_general(
        selected_entries, tokens, (((0,), (0,)), ((), ())), preferred_element_type=jnp.float32
    )
    dispatched_rows = dispatched_rows.astype(jnp.bfloat16).reshape(ranks_ep, capacity, width)
    weight_gate = gate_w[0]
    weight_up = up_w[0]
    weight_down = down_w[0]
    arrived = lax.all_to_all(dispatched_rows, "ep", split_axis=0, concat_axis=0, tiled=True)
    piece = lax.all_gather(arrived[None], ("dp", "tp"), axis=0, tiled=True)
    piece_rows = piece.reshape(-1, width)
    gate = jnp.dot(piece_rows, weight_gate, preferred_element_type=jnp.float32)
    upward = jnp.dot(piece_rows, weight_up, preferred_element_type=jnp.float32)
    hidden_piece = (jax.nn.silu(gate) * upward).astype(jnp.bfloat16)
    hidden = hidden_piece.reshape(piece.shape[:-1] + (weight_gate.shape[1],))
    group_size = hidden.shape[0]
    total_rows = group_size * slots_all
    output_column_slice = weight_down.shape[1]
    summed = jnp.dot(
        lax.all_gather(hidden, ("dp", "tp"), axis=3, tiled=True).reshape(total_rows, -1),
        weight_down,
        preferred_element_type=jnp.float32,
    )
    expert_out = summed.astype(jnp.bfloat16)
    full_rows = lax.all_to_all(
        expert_out.reshape(group_size, slots_all, output_column_slice),
        ("dp", "tp"),
        split_axis=0,
        concat_axis=2,
        tiled=True,
    )
    returned = lax.all_to_all(
        full_rows.reshape(ranks_ep, capacity, width), "ep", split_axis=0, concat_axis=0, tiled=True
    )
    returned_rows = returned.reshape(slots_all, width)
    mixed = jnp.zeros((token_rows, width), jnp.float32)
    for route in range(top_routes):
        chosen_rows = jnp.dot(
            places[:, route].astype(jnp.bfloat16), returned_rows, preferred_element_type=jnp.float32
        )
        mixed = mixed + gates[:, route : route + 1] * chosen_rows
    return (attn_out, mixed.astype(jnp.bfloat16))


MESH = pl.DeviceIdType.MESH
PLANE = 8
LAYERS = 4


def window_kernel(
    tables_ref,
    lengths_ref,
    mig_dst_ref,
    mig_seq_ref,
    queries_ref,
    cache_ref,
    pages_ref,
    tokens_ref,
    gate_w_ref,
    up_w_ref,
    down_w_ref,
    attn_ref,
    ret,
    tok,
    hid,
    out,
    wg,
    wu,
    wd,
    qry,
    pool,
    moved,
    part,
    part_in,
    stat,
    stat_in,
    loc_sem,
    zs,
    zr,
    ts,
    tr,
    hs,
    hr,
    os_,
    or_,
    qs,
    qr,
    ms,
    ps,
    pr,
    ss,
    sr,
):
    x = lax.axis_index("dp")
    t = lax.axis_index("tp")
    z = lax.axis_index("ep")
    y = lax.div(t, 2)
    c = lax.rem(t, 2)
    me = x * 4 + t
    ax, ay = lax.rem(x + 1 + c, 2), lax.rem(y + c, 2)
    bx, by = lax.rem(x + c, 2), lax.rem(y + 1 + c, 2)
    at, bt, st = ay * 2 + c, by * 2 + c, y * 2 + (1 - c)
    dev_a, dev_b, dev_s = (ax, at, z), (bx, bt, z), (x, st, z)
    dt = (1 - y) * 2 + c
    id_a, id_b, id_d = ax * 4 + at, bx * 4 + bt, (1 - x) * 4 + dt
    flip = 1 - 2 * c
    z_pair = lax.div(z, 2) * 2 + lax.rem(z + 1, 2)
    inner = lax.div(z + 1, 2) == 1

    half = lax.div(z, 2)

    def layer(i):
        first, last = lax.div(3 - i, 3), lax.div(i, 3)
        middle = 1 - first - last
        other = (2 - i) * (2 - half) + (i - 1) * (3 - 3 * half)
        return first * z + middle * other + last * z_pair

    def remote(src, dst, send, recv, device):
        return pltpu.make_async_remote_copy(
            src_ref=src,
            dst_ref=dst,
            send_sem=send,
            recv_sem=recv,
            device_id=device,
            device_id_type=MESH,
        )

    barrier = pltpu.get_barrier_semaphore()
    world = PLANE * LAYERS

    def greet(j, carry):
        number = lax.rem(me * LAYERS + z + j, world)
        pl.semaphore_signal(
            barrier,
            inc=1,
            device_id=(
                lax.div(number, 16),
                lax.rem(lax.div(number, LAYERS), 4),
                lax.rem(number, LAYERS),
            ),
            device_id_type=MESH,
        )
        return carry

    own_block = tok.at[z, me]
    local = [
        pltpu.make_async_copy(tokens_ref, own_block, loc_sem.at[0]),
        pltpu.make_async_copy(queries_ref, qry.at[t], loc_sem.at[1]),
        pltpu.make_async_copy(cache_ref, pool, loc_sem.at[2]),
        pltpu.make_async_copy(gate_w_ref.at[0], wg, loc_sem.at[3]),
        pltpu.make_async_copy(up_w_ref.at[0], wu, loc_sem.at[4]),
        pltpu.make_async_copy(down_w_ref.at[0], wd, loc_sem.at[5]),
    ]
    for copy in local:
        copy.start()
    lax.fori_loop(1, world, greet, 0)
    pl.semaphore_wait(barrier, world - 1)

    def to_a(buf, k, send, recv):
        return remote(buf.at[k, me], buf.at[k, me], send.at[k, 0], recv.at[k, 0], dev_a)

    def to_b(buf, k, send, recv):
        return remote(buf.at[k, me], buf.at[k, me], send.at[k, 1], recv.at[k, 1], dev_b)

    def on_b(buf, k, send, recv):
        return remote(buf.at[k, id_a], buf.at[k, id_a], send.at[k, 2], recv.at[k, 2], dev_b)

    def to_s(buf, k, send, recv, n, ident):
        return remote(
            buf.at[k, ident], buf.at[k, ident], send.at[k, 3 + n], recv.at[k, 3 + n], dev_s
        )

    def from_s(buf, k, send, recv, n, ident):
        other = ident + flip
        return remote(
            buf.at[k, other], buf.at[k, other], send.at[k, 3 + n], recv.at[k, 3 + n], dev_s
        )

    def arrived(buf, k, send, recv, n, ident):
        return remote(buf.at[k, ident], buf.at[k, ident], send.at[k, n], recv.at[k, n], dev_a)

    def cast_start(*group, plane=True):
        @pl.when(plane)
        def _():
            to_a(*group).start()
            to_b(*group).start()

        to_s(*group, 0, me).start()

    def cast_forward(*group, plane=True):
        arrived(*group, 0, id_a).wait_recv()

        @pl.when(plane)
        def _():
            on_b(*group).start()

        to_s(*group, 1, id_a).start()
        arrived(*group, 1, id_b).wait_recv()
        to_s(*group, 2, id_b).start()

    def cast_end(*group):
        arrived(*group, 2, id_d).wait_recv()
        to_s(*group, 3, id_d).start()
        for n, ident in enumerate((me, id_b, id_a, id_d)):
            from_s(*group, n, ident).wait_recv()

    def cast_sent(*group):
        to_a(*group).wait_send()
        to_b(*group).wait_send()
        on_b(*group).wait_send()
        for n, ident in enumerate((me, id_a, id_b, id_d)):
            to_s(*group, n, ident).wait_send()

    def tok_group(i):
        return (tok, layer(i), ts, tr)

    def hid_group(i):
        return (hid, layer(i), hs, hr)

    def z_copy(k, n, target):
        return remote(tok.at[k, me], tok.at[k, me], zs.at[k, n], zr.at[k], (x, t, target))

    def pair_copy(n, ident):
        return remote(
            tok.at[z, ident], tok.at[z, ident], ts.at[z_pair, n], tr.at[z, n], (x, t, z_pair)
        )

    def out_copy(k, p):
        return remote(
            out.at[k, p],
            ret.at[z, me],
            os_.at[k, p],
            or_.at[z, me],
            (lax.div(p, 4), lax.rem(p, 4), k),
        )

    def out_send(i):
        k = layer(i)

        def send(j, carry):
            out_copy(k, lax.rem(me + j, PLANE)).start()
            return carry

        lax.fori_loop(lax.div(3 - i, 3), PLANE, send, 0)

    local[0].wait()
    z_copy(z, 0, z_pair).start()

    @pl.when(inner)
    def _():
        z_copy(z, 1, 3 - z).start()

    y_dev, x_dev = (x, dt, z), (1 - x, t, z)
    local[1].wait()
    q_far = remote(qry.at[t], qry.at[t], qs.at[0], qr.at[0], y_dev)
    q_near = remote(qry.at[t], qry.at[t], qs.at[1], qr.at[1], dev_s)
    q_far.start()
    q_near.start()
    page_copy = remote(pages_ref, moved, ms.at[0], ms.at[1], x_dev)
    q_pass = remote(qry.at[dt], qry.at[dt], qs.at[2], qr.at[2], dev_s)
    sd = (1 - y) * 2 + (1 - c)

    def part_copies(n):
        u = (st, sd, dt)[n]
        device = (dev_s, dev_s, y_dev)[n]
        return (
            remote(part.at[u], part_in.at[n], ps.at[n], pr.at[n], device),
            remote(stat.at[u], stat_in.at[n], ss.at[n], sr.at[n], device),
        )

    def merge(mine, slots):
        tops = [stat[mine, :, 0:3]] + [stat_in[n, :, 0:3] for n in slots]
        sums = [stat[mine, :, 3:6]] + [stat_in[n, :, 3:6] for n in slots]
        most = functools.reduce(jnp.maximum, tops)
        factors = [jnp.exp(top - most) for top in tops]
        denominator = sum(f * a for f, a in zip(factors, sums))
        numerators = []
        for s in range(3):
            value = factors[0][:, s : s + 1] * part[mine, s].astype(jnp.float32)
            for factor, n in zip(factors[1:], slots):
                value = value + factor[:, s : s + 1] * part_in[n, s].astype(jnp.float32)
            numerators.append(value)
        return most, denominator, numerators

    def pass_on():
        for copy in part_copies(1):
            copy.wait_recv()
        most, denominator, numerators = merge(dt, (1,))
        stat[dt, :, 0:3] = most
        stat[dt, :, 3:6] = denominator
        for s in range(3):
            part[dt, s] = numerators[s].astype(jnp.bfloat16)
        for copy in part_copies(2):
            copy.start()

    def attend():
        remote(qry.at[st], qry.at[st], qs.at[1], qr.at[1], dev_s).wait_recv()
        remote(qry.at[sd], qry.at[sd], qs.at[2], qr.at[2], dev_s).wait_recv()
        local[2].wait()
        page_copy.wait_recv()
        receives = mig_dst_ref[0] == x
        lane = lax.broadcasted_iota(jnp.int32, (HEADS_ALL, 128), 1)
        stats = jnp.zeros((HEADS_ALL, 128), jnp.float32)
        for s in range(3):
            chosen = receives & (mig_seq_ref[0] == s)
            query = qry[:, s].reshape(HEADS_ALL, KV_RANK + ROPE_DIM)
            pages, masked = [], []
            for j in range(SLOTS):
                page = jnp.where(chosen, moved[j], pool[tables_ref[0, s * SLOTS + j]])
                score = (
                    lax.dot_general(
                        query, page, (((1,), (0,)), ((), ())), preferred_element_type=jnp.float32
                    )
                    * score_scale
                )
                position = (j * 4 + t) * PAGE + lax.broadcasted_iota(
                    jnp.int32, (HEADS_ALL, PAGE), 1
                )
                valid = position < lengths_ref[0, 0, s]
                pages.append((page, valid))
                masked.append(jnp.where(valid, score, neg_fill))
            top = jnp.max(jnp.maximum(masked[0], masked[1]), axis=1, keepdims=True)
            total = jnp.zeros((HEADS_ALL, 1), jnp.float32)
            acc = jnp.zeros((HEADS_ALL, KV_RANK), jnp.float32)
            for j in range(SLOTS):
                page, valid = pages[j]
                weight = jnp.where(valid, jnp.exp(masked[j] - top), 0.0).astype(jnp.bfloat16)
                total = total + jnp.sum(weight.astype(jnp.float32), axis=1, keepdims=True)
                acc = acc + lax.dot_general(
                    weight,
                    page[:KV_RANK],
                    (((1,), (1,)), ((), ())),
                    preferred_element_type=jnp.float32,
                )
            stats = jnp.where(lane == s, top, stats)
            stats = jnp.where(lane == 3 + s, total, stats)
            part[:, s] = acc.astype(jnp.bfloat16).reshape(4, HEADS_ALL // 4, KV_RANK)
        stat[...] = stats.reshape(4, HEADS_ALL // 4, 128)
        for n in (1, 0):
            for copy in part_copies(n):
                copy.start()

    def step(i, carry):
        @pl.when(i == 0)
        def _():
            cast_start(*tok_group(0))

        @pl.when((i > 0) & (i < 4))
        def _():
            k = layer(i)

            @pl.when(i < 3)
            def _():
                z_copy(k, 0, z_pair).wait_recv()

                @pl.when(inner)
                def _():
                    z_copy(k, 0, z_pair).start()

            @pl.when(i == 1)
            def _():
                z_copy(z_pair, 0, z_pair).wait_recv()

                @pl.when(inner)
                def _():
                    z_copy(z_pair, 0, 3 - z).start()

            cast_start(*tok_group(i), plane=i < 3)

        @pl.when((i > 0) & (i < 5))
        def _():
            cast_forward(*tok_group(i - 1), plane=i < 4)

        @pl.when(i == 1)
        def _():
            remote(qry.at[dt], qry.at[dt], qs.at[0], qr.at[0], y_dev).wait_recv()
            q_pass.start()

        @pl.when(i == 3)
        def _():
            page_copy.start()

        @pl.when(i == 2)
        def _():
            local[3].wait()
            local[4].wait()
            local[5].wait()

        @pl.when((i > 1) & (i < 6))
        def _():
            cast_end(*tok_group(i - 2))

            @pl.when(i == 2)
            def _():
                for n, ident in enumerate((id_a, id_b, id_d)):
                    pair_copy(n, ident).start()

            k = layer(i - 2)
            rows = tok[k].reshape(PLANE * 16, tok.shape[3])
            gate = jnp.dot(rows, wg[...], preferred_element_type=jnp.float32)
            up = jnp.dot(rows, wu[...], preferred_element_type=jnp.float32)
            hid[k, me] = (gate / (1.0 + jnp.exp(-gate)) * up).astype(jnp.bfloat16)
            cast_start(*hid_group(i - 2))

        @pl.when(i == 6)
        def _():
            attend()

        @pl.when(i == 7)
        def _():
            pass_on()

        @pl.when((i > 2) & (i < 7))
        def _():
            cast_forward(*hid_group(i - 3))

        @pl.when(i > 3)
        def _():
            cast_end(*hid_group(i - 4))
            k = layer(i - 4)
            depth = hid.shape[3]
            total = jnp.zeros((PLANE * 16, out.shape[3]), jnp.float32)
            for p in range(PLANE):
                total = total + lax.dot_general(
                    hid[k, p],
                    wd[:, p * depth : (p + 1) * depth],
                    (((1,), (1,)), ((), ())),
                    preferred_element_type=jnp.float32,
                )
            out[k] = total.astype(jnp.bfloat16).reshape(PLANE, 16, out.shape[3])
            out_send(i - 4)

        return carry

    lax.fori_loop(0, 8, step, 0)
    keep = pltpu.make_async_copy(out.at[z, me], ret.at[z, me], loc_sem.at[6])
    keep.start()

    for n in (0, 2):
        for copy in part_copies(n):
            copy.wait_recv()
    most, denominator, numerators = merge(t, (0, 2))
    for s in range(3):
        attn_ref[s] = (numerators[s] / denominator[:, s : s + 1]).astype(jnp.bfloat16)

    q_far.wait_send()
    q_near.wait_send()
    q_pass.wait_send()
    page_copy.wait_send()
    for n in range(3):
        for copy in part_copies(n):
            copy.wait_send()
    z_copy(z, 0, z_pair).wait_send()

    @pl.when(inner)
    def _():
        z_copy(z, 1, 3 - z).wait_send()

    def drain(i, carry):
        @pl.when((i > 0) & inner)
        def _():
            z_copy(layer(i), 0, z_pair).wait_send()

        cast_sent(*tok_group(i))
        cast_sent(*hid_group(i))
        return carry

    lax.fori_loop(0, 4, drain, 0)

    def out_wait(i, carry):
        k = layer(i)

        def one(j, inside):
            p = lax.rem(me + j, PLANE)
            out_copy(k, p).wait_send()
            remote(out.at[k, p], ret.at[k, p], os_.at[k, p], or_.at[k, p], dev_s).wait_recv()
            return inside

        return lax.fori_loop(lax.div(3 - i, 3), PLANE, one, carry)

    lax.fori_loop(0, 4, out_wait, 0)
    keep.wait()


def mix_kernel(raw_ref, ret, routes_ref, gates_ref, attn_ref, moe_ref):
    attn_ref[...] = raw_ref[...]
    named, scale = routes_ref[...], gates_ref[...]
    count = named.shape[1]
    same = lax.broadcasted_iota(jnp.int32, (count, count), 0) == lax.broadcasted_iota(
        jnp.int32, (count, count), 1
    )
    coefs = []
    for e in range(LAYERS):
        hits = jnp.sum(jnp.where(named == e, scale, 0.0), axis=0, keepdims=True)
        coefs.append(jnp.sum(jnp.where(same, hits, 0.0), axis=1, keepdims=True))
    span = ret.shape[3]
    for p in range(PLANE):
        mixed = coefs[0] * ret[0, p].astype(jnp.float32)
        for e in range(1, LAYERS):
            mixed = mixed + coefs[e] * ret[e, p].astype(jnp.float32)
        moe_ref[:, p * span : (p + 1) * span] = mixed.astype(jnp.bfloat16)


HEADS_ALL = 128


def window(
    queries,
    cache,
    tables,
    lengths,
    mig_cache,
    mig_src,
    mig_dst,
    mig_seq,
    tokens,
    routes,
    gates,
    gate_w,
    up_w,
    down_w,
):
    rows, width = tokens.shape
    depth, span, units = gate_w.shape[2], down_w.shape[2], down_w.shape[1]
    heads, row_width = queries.shape[1], queries.shape[2]
    pool, moved = jnp.swapaxes(cache, 1, 2), jnp.swapaxes(mig_cache, 1, 2)
    bf16, f32 = jnp.bfloat16, jnp.float32
    dma = pltpu.SemaphoreType.DMA
    smem = pl.BlockSpec(memory_space=pltpu.SMEM)
    vmem = pl.BlockSpec(memory_space=pltpu.VMEM)
    hbm = pl.BlockSpec(memory_space=pl.ANY)
    raw, returned = pl.pallas_call(
        window_kernel,
        out_shape=(
            jax.ShapeDtypeStruct((queries.shape[0], heads, KV_RANK), bf16),
            jax.ShapeDtypeStruct((LAYERS, PLANE, rows, span), bf16),
        ),
        in_specs=[smem] * 4 + [hbm] * 7,
        out_specs=(vmem, hbm),
        scratch_shapes=[
            pltpu.VMEM((LAYERS, PLANE, rows, width), bf16),
            pltpu.VMEM((LAYERS, PLANE, PLANE * rows, depth), bf16),
            pltpu.VMEM((LAYERS, PLANE, rows, span), bf16),
            pltpu.VMEM((width, depth), bf16),
            pltpu.VMEM((width, depth), bf16),
            pltpu.VMEM((span, units), bf16),
            pltpu.VMEM((4, 3, heads, row_width), bf16),
            pltpu.VMEM(pool.shape, bf16),
            pltpu.VMEM(moved.shape, bf16),
            pltpu.VMEM((4, 3, heads, KV_RANK), bf16),
            pltpu.VMEM((3, 3, heads, KV_RANK), bf16),
            pltpu.VMEM((4, heads, 128), f32),
            pltpu.VMEM((3, heads, 128), f32),
            dma((7,)),
            dma((4, 2)),
            dma((4,)),
            dma((4, 7)),
            dma((4, 7)),
            dma((4, 7)),
            dma((4, 7)),
            dma((4, PLANE)),
            dma((4, PLANE)),
            dma((3,)),
            dma((3,)),
            dma((2,)),
            dma((3,)),
            dma((3,)),
            dma((3,)),
            dma((3,)),
        ],
        compiler_params=pltpu.CompilerParams(
            collective_id=0, has_side_effects=True, vmem_limit_bytes=60 * 1024 * 1024
        ),
    )(
        tables,
        lengths,
        mig_dst,
        mig_seq,
        queries,
        pool,
        moved,
        tokens,
        gate_w,
        up_w,
        jnp.swapaxes(down_w, 1, 2),
    )
    return pl.pallas_call(
        mix_kernel,
        out_shape=(
            jax.ShapeDtypeStruct(raw.shape, bf16),
            jax.ShapeDtypeStruct((rows, width), bf16),
        ),
        in_specs=[vmem] * 4,
        out_specs=(vmem, vmem),
        compiler_params=pltpu.CompilerParams(vmem_limit_bytes=60 * 1024 * 1024),
    )(raw, returned, routes.T, gates.T)


def solution(mesh):
    form = per_device
    if (mesh.shape["dp"], mesh.shape["tp"], mesh.shape["ep"]) == (2, 4, LAYERS):
        form = window
    in_specs = (
        P(("dp", "ep"), "tp", None),
        P(("dp", "tp", "ep"), None, None),
        P(("dp", "tp", "ep"), None),
        P("dp", "ep", None),
        P(("dp", "tp", "ep"), None, None),
        P("ep"),
        P("ep"),
        P("ep"),
        P(("dp", "tp", "ep"), None),
        P(("dp", "tp", "ep"), None),
        P(("dp", "tp", "ep"), None),
        P("ep", None, ("dp", "tp")),
        P("ep", None, ("dp", "tp")),
        P("ep", None, ("dp", "tp")),
    )
    out_specs = (P(("dp", "ep"), "tp", None), P(("dp", "tp", "ep"), None))
    return jax.shard_map(
        form, mesh=mesh, in_specs=in_specs, out_specs=out_specs, check_vma=False
    )
```
